32 devices in a mesh: seq: 8 (over z, y), res: 4 (over x, core).
Axes of the slice: x: 2, y: 2, z: 4, core: 2. Of those that a mesh axis runs over, the one named last changes fastest.
Arguments:
- alignment_embedding: bfloat16 [128, 128, 768], P('seq', 'res'), may hold values from -12 to 12
- probe_projector: bfloat16 [768, 768], replicated, may hold values from -0.21875 to 0.21875
- lookup_projector: bfloat16 [768, 768], replicated, may hold values from -0.21875 to 0.21875
- content_projector: bfloat16 [768, 768], replicated, may hold values from -0.21875 to 0.21875
- final_projector: bfloat16 [768, 768], replicated, may hold values from -0.21875 to 0.21875
Outputs:
- mixed: bfloat16 [128, 128, 768], P('seq', 'res')
The draws below stay inside these ranges and needn't reach their ends.
All inputs are finite; a program needn't handle non-finite values.
Results may differ from the reference program's by a relative error of at most 0.01.
Values may be sent and summed in bfloat16 or wider, within the bound.
No kernel may reach another device: no remote copies, remote signals or barrier semaphores. Data moves between devices by JAX's collectives and lax.ppermute only.
A program may use at most 128 MiB of HBM per device.

```python
import jax
import jax.numpy as jnp
from jax import lax

EMBED_DIM = 768
H = 12
LOCAL_SEQUENCES = 16
R = 128
ALIGNED_SITES = 128
N_SEQ = 8


def draw_alignment_embedding(key, part):
    base = jax.random.normal(jax.random.fold_in(key, 11), (R, ALIGNED_SITES, EMBED_DIM), jnp.float32)
    base = jnp.clip(base, -6.0, 6.0)
    return jnp.clip(base, -12.0, 12.0).astype(jnp.bfloat16)


def centred(key, extent, deviation, limit, dtype=jnp.bfloat16):
    entries = deviation * jax.random.normal(key, extent, jnp.float32)
    return jnp.clip(entries, min=-limit, max=limit).astype(dtype)


def setup_inputs(seed: int = 0) -> dict:
    key_of = jax.random.split(jax.random.key(seed), 6)
    alignment_embedding = draw_alignment_embedding(jax.random.fold_in(key_of[5], 71), 0)
    probe_projector = centred(key_of[1], (EMBED_DIM, EMBED_DIM), EMBED_DIM ** -0.5, 0.21875)
    lookup_projector = centred(key_of[2], (EMBED_DIM, EMBED_DIM), EMBED_DIM ** -0.5, 0.21875)
    content_projector = centred(key_of[3], (EMBED_DIM, EMBED_DIM), EMBED_DIM ** -0.5, 0.21875)
    final_projector = centred(key_of[4], (EMBED_DIM, EMBED_DIM), EMBED_DIM ** -0.5, 0.21875)
    return dict(alignment_embedding=alignment_embedding, probe_projector=probe_projector, lookup_projector=lookup_projector, content_projector=content_projector, final_projector=final_projector)


def project(block, weight):
    flat = block.reshape(-1, EMBED_DIM)
    out = jnp.dot(flat, weight, preferred_element_type=jnp.float32).astype(jnp.bfloat16)
    return out.reshape(block.shape[0], ALIGNED_SITES, H, EMBED_DIM // H)

def reference(alignment_embedding, probe_projector, lookup_projector, content_projector, final_projector):
    tile_groups = alignment_embedding.reshape(N_SEQ, LOCAL_SEQUENCES, ALIGNED_SITES, EMBED_DIM)

    def add_logits(total, block):
        probe_tensor = project(block, probe_projector).astype(jnp.float32)
        lookup_tensor = project(block, lookup_projector).astype(jnp.float32)
        return (total + jnp.einsum('rihe,rjhe->hij', probe_tensor, lookup_tensor), None)
    logits, _ = lax.scan(add_logits, jnp.zeros((H, ALIGNED_SITES, ALIGNED_SITES), jnp.float32), tile_groups)
    logits = logits / jnp.sqrt(jnp.float32(EMBED_DIM // H * R))
    probs = jax.nn.softmax(logits, axis=-1).astype(jnp.bfloat16)

    def finish(block):
        content_tensor = project(block, content_projector).astype(jnp.float32)
        attended = jnp.einsum('hij,rjhe->rihe', probs.astype(jnp.float32), content_tensor).astype(jnp.bfloat16)
        mixed = jnp.dot(attended.reshape(-1, EMBED_DIM), final_projector, preferred_element_type=jnp.float32)
        return mixed.astype(jnp.bfloat16).reshape(LOCAL_SEQUENCES, ALIGNED_SITES, EMBED_DIM)
    return lax.map(finish, tile_groups).reshape(R, ALIGNED_SITES, EMBED_DIM)
```

```python
import functools
import math

import jax
import jax.numpy as jnp
from jax import lax
from jax.experimental import pallas as pl
from jax.experimental.pallas import tpu as pltpu
from jax.sharding import PartitionSpec as P

H = 12
GROUP = 4
F32, BF16 = jnp.float32, jnp.bfloat16


def reshape_by_group(inputs, weight, attention_groups):
    sequence_number, site_number, embed_size = inputs.shape
    out = jnp.dot(
        inputs.reshape(sequence_number * site_number, embed_size),
        weight,
        preferred_element_type=F32,
    )
    return out.astype(BF16).reshape(
        sequence_number, site_number, attention_groups, embed_size // attention_groups
    )


def plain_body(
    alignment_embedding, probe_projector, lookup_projector, content_projector, final_projector
):
    sequence_number, site_number, embed_size = alignment_embedding.shape
    head_size = embed_size // H
    scale = 1.0 / math.sqrt(head_size * sequence_number * lax.axis_size("seq"))
    probe_tensor = reshape_by_group(alignment_embedding, probe_projector, H)
    gathered = lax.all_gather(alignment_embedding, "res", axis=1, tiled=True)
    all_keys = reshape_by_group(gathered, lookup_projector, H)
    all_values = reshape_by_group(gathered, content_projector, H)
    logits = jnp.einsum("rihe,rjhe->hij", probe_tensor, all_keys, preferred_element_type=F32)
    summed = lax.psum(logits, "seq")
    probs = jax.nn.softmax(summed * scale, axis=-1).astype(BF16)
    attended = jnp.einsum("hij,rjhe->rihe", probs, all_values, preferred_element_type=F32)
    attended = attended.astype(BF16).reshape(sequence_number * site_number, embed_size)
    mixed = jnp.dot(attended, final_projector, preferred_element_type=F32).astype(BF16)
    return mixed.reshape(sequence_number, site_number, embed_size)


def call(kernel, outs, args, flops=0, scratch=()):
    shapes = [jax.ShapeDtypeStruct(s, d) for s, d in outs]
    moved = sum(a.size * a.dtype.itemsize for a in list(args) + shapes)
    return pl.pallas_call(
        kernel,
        out_shape=shapes,
        in_specs=[pl.BlockSpec(memory_space=pltpu.VMEM)] * len(args),
        out_specs=[pl.BlockSpec(memory_space=pltpu.VMEM)] * len(shapes),
        scratch_shapes=list(scratch),
        cost_estimate=pl.CostEstimate(flops=flops, bytes_accessed=moved, transcendentals=0),
        compiler_params=pltpu.CompilerParams(vmem_limit_bytes=40 * 1024 * 1024),
    )(*args)


def matmul(x, w):
    return jnp.dot(x, w, preferred_element_type=F32).astype(BF16)


def by_head(block, head_size):
    heads = block.shape[1] // head_size
    lane = lax.broadcasted_iota(jnp.int32, block.shape, 1) // head_size
    zero = jnp.zeros_like(block)
    return jnp.concatenate([jnp.where(lane == h, block, zero) for h in range(heads)], axis=0)


def against(probe, keys):
    return lax.dot_general(probe, keys, (((1,), (1,)), ((), ())), preferred_element_type=F32)


def kernel_near(rows, sites, width, x_own, x_twin, wq, wk, q_out, k_out, logits_out):
    q_out[...] = matmul(x_own[...], wq[...])
    for t, x in enumerate((x_own, x_twin)):
        k = matmul(x[...], wk[...])
        for r in range(rows):
            k_out[r, t * sites : (t + 1) * sites, :] = k[r * sites : (r + 1) * sites, :]
    stack = GROUP * sites
    for g in range(H // GROUP):
        lanes = slice(g * width, (g + 1) * width)
        total = jnp.zeros((stack, 2 * sites), F32)
        for r in range(rows):
            probe = by_head(q_out[r * sites : (r + 1) * sites, lanes], width // GROUP)
            total = total + against(probe, k_out[r, :, lanes])
        logits_out[g * stack : (g + 1) * stack, :] = total


def kernel_far(
    rows, sites, width, x_far, x_far_twin, wq, wk, q_own, k_near, near, *refs
):
    parts, (far_k, far_q, ahead, back) = refs[:GROUP], refs[GROUP:]
    half = rows // 2
    came = (1 - lax.axis_index("res") // 2) * half
    me = lax.rem(lax.axis_index("seq"), GROUP)
    for t, x in enumerate((x_far, x_far_twin)):
        k = matmul(x[...], wk[...])
        for r in range(half):
            far_k[r, t * sites : (t + 1) * sites, :] = k[r * sites : (r + 1) * sites, :]
    far_q[...] = matmul(x_far[...], wq[...])
    stack = GROUP * sites
    for g in range(H // GROUP):
        lanes = slice(g * width, (g + 1) * width)
        one = jnp.zeros((stack, 2 * sites), F32)
        two = jnp.zeros((stack, 2 * sites), F32)
        for r in range(half):
            own = q_own[pl.ds((came + r) * sites, sites), lanes]
            one = one + against(by_head(own, width // GROUP), far_k[r, :, lanes])
            other = far_q[r * sites : (r + 1) * sites, lanes]
            two = two + against(by_head(other, width // GROUP), k_near[came + r, :, lanes])
        rows_g = slice(g * stack, (g + 1) * stack)
        ahead[rows_g, :] = jnp.concatenate([near[rows_g, :], one], axis=1)
        back[rows_g, :] = two
    size = H * sites // GROUP
    for k in range(GROUP):
        at = lax.bitwise_xor(me, k) * size
        parts[k][:size, :] = ahead[pl.ds(at, size), :]
        parts[k][size:, :] = jnp.concatenate(
            [back[pl.ds(at, size // 2), :], back[pl.ds(at + size // 2, size // 2), :]], axis=1
        )


def kernel_sum(size, a, b, c, d, ahead, back):
    ahead[...] = (a[:size, :] + b[:size, :]) + (c[:size, :] + d[:size, :])
    back[...] = (a[size:, :] + b[size:, :]) + (c[size:, :] + d[size:, :])


def kernel_softmax(scale, ahead, ahead_z, back_x, back_xz, out):
    far = back_x[...] + back_xz[...]
    half = far.shape[1] // 2
    far = jnp.concatenate([far[:, :half], far[:, half:]], axis=0)
    far = jnp.concatenate([jnp.zeros_like(far), far], axis=1)
    logits = (ahead[...] + ahead_z[...] + far) * scale
    e = jnp.exp(logits - jnp.max(logits, axis=1, keepdims=True))
    out[...] = (e / jnp.sum(e, axis=1, keepdims=True)).astype(BF16)


def kernel_values(sites, *refs):
    w, outs = refs[-1 - (len(refs) - 1) // 3], refs[-((len(refs) - 1) // 3) :]
    for n, out in enumerate(outs):
        for t in range(2):
            v = matmul(refs[2 * n + t][...], w[...])
            for r in range(out.shape[0]):
                out[r, t * sites : (t + 1) * sites, :] = v[r * sites : (r + 1) * sites, :]


def kernel_last(rows, sites, width, p0, p1, p2, p3, v_near, v_first, v_second, wo, out, probs, att):
    half = rows // 2
    place = lax.axis_index("res") // 2
    me = lax.rem(lax.axis_index("seq"), GROUP)
    size = H * sites // GROUP
    for k, p in enumerate((p0, p1, p2, p3)):
        probs[pl.ds(lax.bitwise_xor(me, k) * size, size), :] = p[...]
    stack, head = GROUP * sites, width // GROUP
    lane = lax.broadcasted_iota(jnp.int32, (sites, width), 1) // head
    for n, (far, start) in enumerate(((v_first, (1 - place) * half), (v_second, place * half))):
        for r in range(half):
            for g in range(H // GROUP):
                lanes = slice(g * width, (g + 1) * width)
                v = jnp.concatenate([v_near[start + r, :, lanes], far[r, :, lanes]], axis=0)
                full = jnp.dot(
                    probs[g * stack : (g + 1) * stack, :], v, preferred_element_type=F32
                )
                one = full[:sites]
                for h in range(1, GROUP):
                    one = jnp.where(lane == h, full[h * sites : (h + 1) * sites], one)
                att[r * sites : (r + 1) * sites, lanes] = one.astype(BF16)
        out[pl.ds(start * sites, half * sites), :] = matmul(att[...], wo[...])


def swap(x, axis, bit):
    count = lax.axis_size(axis)
    return lax.ppermute(x, axis, [(i, i ^ bit) for i in range(count)])


def body(x, wq, wk, wv, wo):
    rows, sites, embed = x.shape
    half, width = rows // 2, embed // (H // GROUP)
    n_seq, n_res = lax.axis_size("seq"), lax.axis_size("res")
    scale = 1.0 / math.sqrt(embed // H * rows * n_seq)
    flat, half_flat = (rows * sites, embed), (half * sites, embed)
    place = lax.axis_index("res") // 2
    own = x.reshape(flat)
    cost = 2 * rows * sites * embed * embed

    sent_first = lax.dynamic_slice_in_dim(own, place * half * sites, half * sites)
    far_first = swap(sent_first, "res", 2)
    twin = swap(own, "res", 1)
    far_first_twin = swap(far_first, "res", 1)
    sent_second = lax.dynamic_slice_in_dim(own, (1 - place) * half * sites, half * sites)
    sent_second, _ = lax.optimization_barrier((sent_second, far_first))
    far_second = swap(sent_second, "res", 2)
    far_second_twin = swap(far_second, "res", 1)

    q, k_near, near = call(
        functools.partial(kernel_near, rows, sites, width),
        [(flat, BF16), ((rows, 2 * sites, embed), BF16), ((H * sites, 2 * sites), F32)],
        (own, twin, wq, wk),
        4 * cost,
    )
    size = H * sites // GROUP
    part = (size + size // 2, 4 * sites)
    parts = call(
        functools.partial(kernel_far, rows, sites, width),
        [(part, F32)] * GROUP,
        (far_first, far_first_twin, wq, wk, q, k_near, near),
        2 * cost,
        [
            pltpu.VMEM((half, 2 * sites, embed), BF16),
            pltpu.VMEM(half_flat, BF16),
            pltpu.VMEM((H * sites, 4 * sites), F32),
            pltpu.VMEM((H * sites, 2 * sites), F32),
        ],
    )
    came = [swap(parts[k], "seq", k) for k in range(1, GROUP)]
    ahead, back = call(
        functools.partial(kernel_sum, size),
        [((size, 4 * sites), F32), ((size // 2, 4 * sites), F32)],
        (parts[0], *came),
    )
    ahead_z = swap(ahead, "seq", GROUP)
    back_x = swap(back, "res", 2)
    cross = [
        (s * n_res + r, (s ^ GROUP) * n_res + (r ^ 2)) for s in range(n_seq) for r in range(n_res)
    ]
    back_xz = lax.ppermute(back, ("seq", "res"), cross)
    (probs,) = call(
        functools.partial(kernel_softmax, scale),
        [((size, 4 * sites), BF16)],
        (ahead, ahead_z, back_x, back_xz),
    )
    others = [swap(probs, "seq", k) for k in range(1, GROUP)]

    v_near, v_first = call(
        functools.partial(kernel_values, sites),
        [((rows, 2 * sites, embed), BF16), ((half, 2 * sites, embed), BF16)],
        (own, twin, far_first, far_first_twin, wv),
        3 * cost,
    )
    (v_second,) = call(
        functools.partial(kernel_values, sites),
        [((half, 2 * sites, embed), BF16)],
        (far_second, far_second_twin, wv),
        cost,
    )
    (out,) = call(
        functools.partial(kernel_last, rows, sites, width),
        [(flat, BF16)],
        (probs, *others, v_near, v_first, v_second, wo),
        2 * cost,
        [pltpu.VMEM((H * sites, 4 * sites), BF16), pltpu.VMEM(half_flat, BF16)],
    )
    return out.reshape(rows, sites, embed)


def solution(mesh):
    placed = (P("seq", "res", None), P(), P(), P(), P())
    fits = mesh.shape["res"] == 4 and mesh.shape["seq"] == 2 * GROUP
    return jax.shard_map(
        body if fits else plain_body,
        mesh=mesh,
        in_specs=placed,
        out_specs=P("seq", "res", None),
        check_vma=False,
    )
```

```python
import functools
import math

import jax
import jax.numpy as jnp
from jax import lax
from jax.experimental import pallas as pl
from jax.experimental.pallas import tpu as pltpu
from jax.sharding import PartitionSpec as P

H = 12
GROUP = 4
F32, BF16 = jnp.float32, jnp.bfloat16


def reshape_by_group(inputs, weight, attention_groups):
    sequence_number, site_number, embed_size = inputs.shape
    out = jnp.dot(
        inputs.reshape(sequence_number * site_number, embed_size),
        weight,
        preferred_element_type=F32,
    )
    return out.astype(BF16).reshape(
        sequence_number, site_number, attention_groups, embed_size // attention_groups
    )


def plain_body(
    alignment_embedding, probe_projector, lookup_projector, content_projector, final_projector
):
    sequence_number, site_number, embed_size = alignment_embedding.shape
    head_size = embed_size // H
    scale = 1.0 / math.sqrt(head_size * sequence_number * lax.axis_size("seq"))
    probe_tensor = reshape_by_group(alignment_embedding, probe_projector, H)
    gathered = lax.all_gather(alignment_embedding, "res", axis=1, tiled=True)
    all_keys = reshape_by_group(gathered, lookup_projector, H)
    all_values = reshape_by_group(gathered, content_projector, H)
    logits = jnp.einsum("rihe,rjhe->hij", probe_tensor, all_keys, preferred_element_type=F32)
    summed = lax.psum(logits, "seq")
    probs = jax.nn.softmax(summed * scale, axis=-1).astype(BF16)
    attended = jnp.einsum("hij,rjhe->rihe", probs, all_values, preferred_element_type=F32)
    attended = attended.astype(BF16).reshape(sequence_number * site_number, embed_size)
    mixed = jnp.dot(attended, final_projector, preferred_element_type=F32).astype(BF16)
    return mixed.reshape(sequence_number, site_number, embed_size)


def call(kernel, outs, args, flops=0, scratch=(), space=pltpu.VMEM):
    shapes = [jax.ShapeDtypeStruct(s, d) for s, d in outs]
    if space == pltpu.HBM:
        args = [pltpu.with_memory_space_constraint(a, space) for a in args]
    moved = sum(a.size * a.dtype.itemsize for a in list(args) + shapes)
    return pl.pallas_call(
        kernel,
        out_shape=shapes,
        in_specs=[pl.BlockSpec(memory_space=space)] * len(args),
        out_specs=[pl.BlockSpec(memory_space=pltpu.VMEM)] * len(shapes),
        scratch_shapes=list(scratch),
        cost_estimate=pl.CostEstimate(flops=flops, bytes_accessed=moved, transcendentals=0),
        compiler_params=pltpu.CompilerParams(vmem_limit_bytes=4 * 1024 * 1024),
    )(*args)


def matmul(x, w):
    return jnp.dot(x, w, preferred_element_type=F32).astype(BF16)


def by_head(block, head_size):
    heads = block.shape[1] // head_size
    lane = lax.broadcasted_iota(jnp.int32, block.shape, 1) // head_size
    zero = jnp.zeros_like(block)
    return jnp.concatenate([jnp.where(lane == h, block, zero) for h in range(heads)], axis=0)


def against(probe, keys):
    return lax.dot_general(probe, keys, (((1,), (1,)), ((), ())), preferred_element_type=F32)


def places(rows, sites, embed):
    counts = dict(q=rows * sites, k=2 * rows * sites, v=2 * rows * sites, near=H * sites)
    counts.update(wq=embed, wk=embed, wv=embed)
    at, start = {}, 0
    for name, count in counts.items():
        at[name] = start
        start += count
    return at, start


def thirds(x):
    high = x.astype(BF16)
    rest = x - high.astype(F32)
    middle = rest.astype(BF16)
    return high, middle, (rest - middle.astype(F32)).astype(BF16)


def kernel_part(count, other, x, out, sem):
    place = lax.axis_index("res") // 2
    start = (1 - place if other else place) * count
    copy = pltpu.make_async_copy(x.at[pl.ds(start, count)], out, sem)
    copy.start()
    copy.wait()


def kernel_near(rows, sites, width, own, twin, wq, wk, wv, kept, x_own, x_twin, sems):
    embed = wq.shape[0]
    at, _ = places(rows, sites, embed)
    copies = {}
    moves = [("own", own, x_own), ("twin", twin, x_twin)]
    moves += [(n, w, kept.at[pl.ds(at[n], embed)]) for n, w in (("wq", wq), ("wk", wk), ("wv", wv))]
    for n, (name, source, target) in enumerate(moves):
        copies[name] = pltpu.make_async_copy(source, target, sems.at[n])
    for name in ("wq", "own", "wk", "twin", "wv"):
        copies[name].start()
    copies["own"].wait()
    copies["wq"].wait()
    kept[at["q"] : at["q"] + rows * sites, :] = matmul(x_own[...], kept[at["wq"] : at["wq"] + embed, :])
    copies["wk"].wait()
    copies["twin"].wait()

    def both(weight, start):
        for t, x in enumerate((x_own, x_twin)):
            y = matmul(x[...], kept[at[weight] : at[weight] + embed, :])
            for r in range(rows):
                to = start + (2 * r + t) * sites
                kept[to : to + sites, :] = y[r * sites : (r + 1) * sites, :]

    both("wk", at["k"])
    copies["wv"].wait()
    both("wv", at["v"])
    stack = GROUP * sites
    for g in range(H // GROUP):
        lanes = slice(g * width, (g + 1) * width)
        total = jnp.zeros((stack, 2 * sites), F32)
        for r in range(rows):
            q = kept[at["q"] + r * sites : at["q"] + (r + 1) * sites, lanes]
            k = kept[at["k"] + 2 * r * sites : at["k"] + 2 * (r + 1) * sites, lanes]
            total = total + against(by_head(q, width // GROUP), k)
        here = slice(at["near"] + g * stack, at["near"] + (g + 1) * stack)
        for n, part in enumerate(thirds(total)):
            kept[here, n * 2 * GROUP * sites : n * 2 * GROUP * sites + 2 * sites] = part


def kernel_far(rows, sites, width, x_far, x_far_twin, kept, *refs):
    parts, (far_k, far_q, ahead, back) = refs[:GROUP], refs[GROUP:]
    embed, half = x_far.shape[1], rows // 2
    at, _ = places(rows, sites, embed)
    came = (1 - lax.axis_index("res") // 2) * half
    me = lax.rem(lax.axis_index("seq"), GROUP)
    for t, x in enumerate((x_far, x_far_twin)):
        k = matmul(x[...], kept[at["wk"] : at["wk"] + embed, :])
        for r in range(half):
            far_k[r, t * sites : (t + 1) * sites, :] = k[r * sites : (r + 1) * sites, :]
    far_q[...] = matmul(x_far[...], kept[at["wq"] : at["wq"] + embed, :])
    stack = GROUP * sites
    for g in range(H // GROUP):
        lanes = slice(g * width, (g + 1) * width)
        one = jnp.zeros((stack, 2 * sites), F32)
        two = jnp.zeros((stack, 2 * sites), F32)
        for r in range(half):
            own = kept[pl.ds(at["q"] + (came + r) * sites, sites), lanes]
            one = one + against(by_head(own, width // GROUP), far_k[r, :, lanes])
            other = far_q[r * sites : (r + 1) * sites, lanes]
            k = kept[pl.ds(at["k"] + 2 * (came + r) * sites, 2 * sites), lanes]
            two = two + against(by_head(other, width // GROUP), k)
        rows_g = slice(g * stack, (g + 1) * stack)
        here = slice(at["near"] + g * stack, at["near"] + (g + 1) * stack)
        near = [
            kept[here, n * 2 * GROUP * sites : n * 2 * GROUP * sites + 2 * sites].astype(F32)
            for n in range(3)
        ]
        ahead[rows_g, :] = jnp.concatenate([near[0] + near[1] + near[2], one], axis=1)
        back[rows_g, :] = two
    size = H * sites // GROUP
    for k in range(GROUP):
        to = lax.bitwise_xor(me, k) * size
        parts[k][:size, :] = ahead[pl.ds(to, size), :]
        parts[k][size:, :] = jnp.concatenate(
            [back[pl.ds(to, size // 2), :], back[pl.ds(to + size // 2, size // 2), :]], axis=1
        )


def kernel_sum(size, a, b, c, d, ahead, back):
    ahead[...] = (a[:size, :] + b[:size, :]) + (c[:size, :] + d[:size, :])
    back[...] = (a[size:, :] + b[size:, :]) + (c[size:, :] + d[size:, :])


def kernel_softmax(scale, ahead, ahead_z, back_x, back_xz, out):
    far = back_x[...] + back_xz[...]
    half = far.shape[1] // 2
    far = jnp.concatenate([far[:, :half], far[:, half:]], axis=0)
    far = jnp.concatenate([jnp.zeros_like(far), far], axis=1)
    logits = (ahead[...] + ahead_z[...] + far) * scale
    e = jnp.exp(logits - jnp.max(logits, axis=1, keepdims=True))
    out[...] = (e / jnp.sum(e, axis=1, keepdims=True)).astype(BF16)


def kernel_values(sites, start, x, x_twin, kept, out):
    w = kept[start : start + x.shape[1], :]
    for t, block in enumerate((x, x_twin)):
        v = matmul(block[...], w)
        for r in range(out.shape[0]):
            out[r, t * sites : (t + 1) * sites, :] = v[r * sites : (r + 1) * sites, :]


def kernel_last(rows, sites, width, p0, p1, p2, p3, kept, v_first, v_second, wo, out, probs, att):
    half = rows // 2
    at, _ = places(rows, sites, wo.shape[0])
    place = lax.axis_index("res") // 2
    me = lax.rem(lax.axis_index("seq"), GROUP)
    size = H * sites // GROUP
    for k, p in enumerate((p0, p1, p2, p3)):
        probs[pl.ds(lax.bitwise_xor(me, k) * size, size), :] = p[...]
    stack, head = GROUP * sites, width // GROUP
    lane = lax.broadcasted_iota(jnp.int32, (sites, width), 1) // head
    for n, (far, start) in enumerate(((v_first, (1 - place) * half), (v_second, place * half))):
        for r in range(half):
            for g in range(H // GROUP):
                lanes = slice(g * width, (g + 1) * width)
                near = kept[pl.ds(at["v"] + 2 * (start + r) * sites, 2 * sites), lanes]
                v = jnp.concatenate([near, far[r, :, lanes]], axis=0)
                full = jnp.dot(
                    probs[g * stack : (g + 1) * stack, :], v, preferred_element_type=F32
                )
                one = full[:sites]
                for h in range(1, GROUP):
                    one = jnp.where(lane == h, full[h * sites : (h + 1) * sites], one)
                att[r * sites : (r + 1) * sites, lanes] = one.astype(BF16)
        out[pl.ds(start * sites, half * sites), :] = matmul(att[...], wo[...])


def swap(x, axis, bit):
    count = lax.axis_size(axis)
    return lax.ppermute(x, axis, [(i, i ^ bit) for i in range(count)])


def body(x, wq, wk, wv, wo):
    rows, sites, embed = x.shape
    half, width = rows // 2, embed // (H // GROUP)
    n_seq, n_res = lax.axis_size("seq"), lax.axis_size("res")
    scale = 1.0 / math.sqrt(embed // H * rows * n_seq)
    flat, half_flat = (rows * sites, embed), (half * sites, embed)
    own = x.reshape(flat)
    cost = 2 * rows * sites * embed * embed

    def part(x, other):
        return call(
            functools.partial(kernel_part, half * sites, other),
            [(half_flat, BF16)],
            (x,),
            scratch=[pltpu.SemaphoreType.DMA],
            space=pltpu.HBM,
        )[0]

    sent_first = part(own, False)
    far_first = swap(sent_first, "res", 2)
    later, sent_first = lax.optimization_barrier((own, sent_first))
    sent_second = part(later, True)
    far_second = swap(sent_second, "res", 2)
    twin = swap(own, "res", 1)
    at, total = places(rows, sites, embed)
    (kept,) = call(
        functools.partial(kernel_near, rows, sites, width),
        [((total, embed), BF16)],
        (own, twin, wq, wk, wv),
        6 * cost,
        [pltpu.VMEM(flat, BF16), pltpu.VMEM(flat, BF16), pltpu.SemaphoreType.DMA((5,))],
        pltpu.HBM,
    )
    far_first, kept = lax.optimization_barrier((far_first, kept))
    far_first_twin = swap(far_first, "res", 1)
    size = H * sites // GROUP
    part = (size + size // 2, 4 * sites)
    parts = call(
        functools.partial(kernel_far, rows, sites, width),
        [(part, F32)] * GROUP,
        (far_first, far_first_twin, kept),
        2 * cost,
        [
            pltpu.VMEM((half, 2 * sites, embed), BF16),
            pltpu.VMEM(half_flat, BF16),
            pltpu.VMEM((H * sites, 4 * sites), F32),
            pltpu.VMEM((H * sites, 2 * sites), F32),
        ],
    )
    came = [swap(parts[k], "seq", k) for k in range(1, GROUP)]
    ahead, back = call(
        functools.partial(kernel_sum, size),
        [((size, 4 * sites), F32), ((size // 2, 4 * sites), F32)],
        (parts[0], *came),
    )
    ahead_z = swap(ahead, "seq", GROUP)
    back_x = swap(back, "res", 2)
    cross = [
        (s * n_res + r, (s ^ GROUP) * n_res + (r ^ 2)) for s in range(n_seq) for r in range(n_res)
    ]
    back_xz = lax.ppermute(back, ("seq", "res"), cross)
    (v_first,) = call(
        functools.partial(kernel_values, sites, at["wv"]),
        [((half, 2 * sites, embed), BF16)],
        (far_first, far_first_twin, kept),
        cost,
    )
    ahead_z, back_x, back_xz, v_first = lax.optimization_barrier((ahead_z, back_x, back_xz, v_first))
    (probs,) = call(
        functools.partial(kernel_softmax, scale),
        [((size, 4 * sites), BF16)],
        (ahead, ahead_z, back_x, back_xz),
    )
    far_second, probs = lax.optimization_barrier((far_second, probs))
    far_second_twin = swap(far_second, "res", 1)
    others = [swap(probs, "seq", k) for k in range(1, GROUP)]

    (v_second,) = call(
        functools.partial(kernel_values, sites, at["wv"]),
        [((half, 2 * sites, embed), BF16)],
        (far_second, far_second_twin, kept),
        cost,
    )
    (out,) = call(
        functools.partial(kernel_last, rows, sites, width),
        [(flat, BF16)],
        (probs, *others, kept, v_first, v_second, wo),
        2 * cost,
        [pltpu.VMEM((H * sites, 4 * sites), BF16), pltpu.VMEM(half_flat, BF16)],
    )
    return out.reshape(rows, sites, embed)


def solution(mesh):
    placed = (P("seq", "res", None), P(), P(), P(), P())
    fits = mesh.shape["res"] == 4 and mesh.shape["seq"] == 2 * GROUP
    return jax.shard_map(
        body if fits else plain_body,
        mesh=mesh,
        in_specs=placed,
        out_specs=P("seq", "res", None),
        check_vma=False,
    )
```

```python
import functools
import math

import jax
import jax.numpy as jnp
from jax import lax
from jax.experimental import pallas as pl
from jax.experimental.pallas import tpu as pltpu
from jax.sharding import PartitionSpec as P

H = 12
GROUP = 4
F32, BF16 = jnp.float32, jnp.bfloat16


def reshape_by_group(inputs, weight, attention_groups):
    sequence_number, site_number, embed_size = inputs.shape
    out = jnp.dot(
        inputs.reshape(sequence_number * site_number, embed_size),
        weight,
        preferred_element_type=F32,
    )
    return out.astype(BF16).reshape(
        sequence_number, site_number, attention_groups, embed_size // attention_groups
    )


def plain_body(
    alignment_embedding, probe_projector, lookup_projector, content_projector, final_projector
):
    sequence_number, site_number, embed_size = alignment_embedding.shape
    head_size = embed_size // H
    scale = 1.0 / math.sqrt(head_size * sequence_number * lax.axis_size("seq"))
    probe_tensor = reshape_by_group(alignment_embedding, probe_projector, H)
    gathered = lax.all_gather(alignment_embedding, "res", axis=1, tiled=True)
    all_keys = reshape_by_group(gathered, lookup_projector, H)
    all_values = reshape_by_group(gathered, content_projector, H)
    logits = jnp.einsum("rihe,rjhe->hij", probe_tensor, all_keys, preferred_element_type=F32)
    summed = lax.psum(logits, "seq")
    probs = jax.nn.softmax(summed * scale, axis=-1).astype(BF16)
    attended = jnp.einsum("hij,rjhe->rihe", probs, all_values, preferred_element_type=F32)
    attended = attended.astype(BF16).reshape(sequence_number * site_number, embed_size)
    mixed = jnp.dot(attended, final_projector, preferred_element_type=F32).astype(BF16)
    return mixed.reshape(sequence_number, site_number, embed_size)


def call(kernel, outs, args, flops=0, scratch=(), space=pltpu.VMEM):
    shapes = [jax.ShapeDtypeStruct(s, d) for s, d in outs]
    if space == pltpu.HBM:
        args = [pltpu.with_memory_space_constraint(a, space) for a in args]
    moved = sum(a.size * a.dtype.itemsize for a in list(args) + shapes)
    return pl.pallas_call(
        kernel,
        out_shape=shapes,
        in_specs=[pl.BlockSpec(memory_space=space)] * len(args),
        out_specs=[pl.BlockSpec(memory_space=pltpu.VMEM)] * len(shapes),
        scratch_shapes=list(scratch),
        cost_estimate=pl.CostEstimate(flops=flops, bytes_accessed=moved, transcendentals=0),
        compiler_params=pltpu.CompilerParams(vmem_limit_bytes=4 * 1024 * 1024),
    )(*args)


def matmul(x, w):
    return jnp.dot(x, w, preferred_element_type=F32).astype(BF16)


def by_head(block, head_size):
    heads = block.shape[1] // head_size
    lane = lax.broadcasted_iota(jnp.int32, block.shape, 1) // head_size
    zero = jnp.zeros_like(block)
    return jnp.concatenate([jnp.where(lane == h, block, zero) for h in range(heads)], axis=0)


def against(probe, keys):
    return lax.dot_general(probe, keys, (((1,), (1,)), ((), ())), preferred_element_type=F32)


def places(rows, sites, embed):
    counts = dict(q=rows * sites, k=2 * rows * sites, v=2 * rows * sites, near=H * sites)
    counts.update(wq=embed, wk=embed, wv=embed)
    at, start = {}, 0
    for name, count in counts.items():
        at[name] = start
        start += count
    return at, start


def thirds(x):
    high = x.astype(BF16)
    rest = x - high.astype(F32)
    middle = rest.astype(BF16)
    return high, middle, (rest - middle.astype(F32)).astype(BF16)


def kernel_part(count, other, x, out, sem):
    place = lax.axis_index("res") // 2
    start = (1 - place if other else place) * count
    copy = pltpu.make_async_copy(x.at[pl.ds(start, count)], out, sem)
    copy.start()
    copy.wait()


def kernel_near(rows, sites, width, own, twin, wq, wk, wv, kept, x_own, x_twin, sems):
    embed = wq.shape[0]
    at, _ = places(rows, sites, embed)
    copies = {}
    moves = [("own", own, x_own), ("twin", twin, x_twin)]
    moves += [(n, w, kept.at[pl.ds(at[n], embed)]) for n, w in (("wq", wq), ("wk", wk), ("wv", wv))]
    for n, (name, source, target) in enumerate(moves):
        copies[name] = pltpu.make_async_copy(source, target, sems.at[n])
    for name in ("wq", "own", "wk", "twin", "wv"):
        copies[name].start()
    copies["own"].wait()
    copies["wq"].wait()
    kept[at["q"] : at["q"] + rows * sites, :] = matmul(x_own[...], kept[at["wq"] : at["wq"] + embed, :])
    copies["wk"].wait()
    copies["twin"].wait()

    def both(weight, start):
        for t, x in enumerate((x_own, x_twin)):
            y = matmul(x[...], kept[at[weight] : at[weight] + embed, :])
            for r in range(rows):
                to = start + (2 * r + t) * sites
                kept[to : to + sites, :] = y[r * sites : (r + 1) * sites, :]

    both("wk", at["k"])
    copies["wv"].wait()
    both("wv", at["v"])
    stack = GROUP * sites
    for g in range(H // GROUP):
        lanes = slice(g * width, (g + 1) * width)
        total = jnp.zeros((stack, 2 * sites), F32)
        for r in range(rows):
            q = kept[at["q"] + r * sites : at["q"] + (r + 1) * sites, lanes]
            k = kept[at["k"] + 2 * r * sites : at["k"] + 2 * (r + 1) * sites, lanes]
            total = total + against(by_head(q, width // GROUP), k)
        here = slice(at["near"] + g * stack, at["near"] + (g + 1) * stack)
        for n, part in enumerate(thirds(total)):
            kept[here, n * 2 * GROUP * sites : n * 2 * GROUP * sites + 2 * sites] = part


def kernel_back(rows, sites, width, x_far, kept, k_far, back, far_q):
    embed, half = x_far.shape[1], rows // 2
    at, _ = places(rows, sites, embed)
    came = (1 - lax.axis_index("res") // 2) * half
    far_q[...] = matmul(x_far[...], kept[at["wq"] : at["wq"] + embed, :])
    k_far[...] = matmul(x_far[...], kept[at["wk"] : at["wk"] + embed, :])
    stack = GROUP * sites
    for g in range(H // GROUP):
        lanes = slice(g * width, (g + 1) * width)
        two = jnp.zeros((stack, 2 * sites), F32)
        for r in range(half):
            other = far_q[r * sites : (r + 1) * sites, lanes]
            k = kept[pl.ds(at["k"] + 2 * (came + r) * sites, 2 * sites), lanes]
            two = two + against(by_head(other, width // GROUP), k)
        back[g * stack : (g + 1) * stack, :] = two


def kernel_ahead(rows, sites, width, x_far_twin, kept, k_far, back, *refs):
    parts, (far_k, ahead) = refs[:GROUP], refs[GROUP:]
    embed, half = x_far_twin.shape[1], rows // 2
    at, _ = places(rows, sites, embed)
    came = (1 - lax.axis_index("res") // 2) * half
    me = lax.rem(lax.axis_index("seq"), GROUP)
    far_k[...] = matmul(x_far_twin[...], kept[at["wk"] : at["wk"] + embed, :])
    stack = GROUP * sites
    for g in range(H // GROUP):
        lanes = slice(g * width, (g + 1) * width)
        one = jnp.zeros((stack, 2 * sites), F32)
        for r in range(half):
            own = kept[pl.ds(at["q"] + (came + r) * sites, sites), lanes]
            row = slice(r * sites, (r + 1) * sites)
            k = jnp.concatenate([k_far[row, lanes], far_k[row, lanes]], axis=0)
            one = one + against(by_head(own, width // GROUP), k)
        here = slice(at["near"] + g * stack, at["near"] + (g + 1) * stack)
        near = [
            kept[here, n * 2 * stack : n * 2 * stack + 2 * sites].astype(F32) for n in range(3)
        ]
        ahead[g * stack : (g + 1) * stack, :] = jnp.concatenate(
            [near[0] + near[1] + near[2], one], axis=1
        )
    size = H * sites // GROUP
    for k in range(GROUP):
        to = lax.bitwise_xor(me, k) * size
        parts[k][:size, :] = ahead[pl.ds(to, size), :]
        parts[k][size:, :] = jnp.concatenate(
            [back[pl.ds(to, size // 2), :], back[pl.ds(to + size // 2, size // 2), :]], axis=1
        )


def kernel_sum(size, a, b, c, d, ahead, back):
    ahead[...] = (a[:size, :] + b[:size, :]) + (c[:size, :] + d[:size, :])
    back[...] = (a[size:, :] + b[size:, :]) + (c[size:, :] + d[size:, :])


def kernel_softmax(scale, ahead, ahead_z, back_x, back_xz, out):
    far = back_x[...] + back_xz[...]
    half = far.shape[1] // 2
    far = jnp.concatenate([far[:, :half], far[:, half:]], axis=0)
    far = jnp.concatenate([jnp.zeros_like(far), far], axis=1)
    logits = (ahead[...] + ahead_z[...] + far) * scale
    e = jnp.exp(logits - jnp.max(logits, axis=1, keepdims=True))
    out[...] = (e / jnp.sum(e, axis=1, keepdims=True)).astype(BF16)


def kernel_values(sites, start, x, x_twin, kept, out):
    w = kept[start : start + x.shape[1], :]
    for t, block in enumerate((x, x_twin)):
        v = matmul(block[...], w)
        for r in range(out.shape[0]):
            out[r, t * sites : (t + 1) * sites, :] = v[r * sites : (r + 1) * sites, :]


def kernel_last(rows, sites, width, p0, p1, p2, p3, kept, v_first, v_second, wo, out, probs, att):
    half = rows // 2
    at, _ = places(rows, sites, wo.shape[0])
    place = lax.axis_index("res") // 2
    me = lax.rem(lax.axis_index("seq"), GROUP)
    size = H * sites // GROUP
    for k, p in enumerate((p0, p1, p2, p3)):
        probs[pl.ds(lax.bitwise_xor(me, k) * size, size), :] = p[...]
    stack, head = GROUP * sites, width // GROUP
    lane = lax.broadcasted_iota(jnp.int32, (sites, width), 1) // head
    for n, (far, start) in enumerate(((v_first, (1 - place) * half), (v_second, place * half))):
        for r in range(half):
            for g in range(H // GROUP):
                lanes = slice(g * width, (g + 1) * width)
                near = kept[pl.ds(at["v"] + 2 * (start + r) * sites, 2 * sites), lanes]
                v = jnp.concatenate([near, far[r, :, lanes]], axis=0)
                full = jnp.dot(
                    probs[g * stack : (g + 1) * stack, :], v, preferred_element_type=F32
                )
                one = full[:sites]
                for h in range(1, GROUP):
                    one = jnp.where(lane == h, full[h * sites : (h + 1) * sites], one)
                att[r * sites : (r + 1) * sites, lanes] = one.astype(BF16)
        out[pl.ds(start * sites, half * sites), :] = matmul(att[...], wo[...])


def swap(x, axis, bit):
    count = lax.axis_size(axis)
    return lax.ppermute(x, axis, [(i, i ^ bit) for i in range(count)])


def body(x, wq, wk, wv, wo):
    rows, sites, embed = x.shape
    half, width = rows // 2, embed // (H // GROUP)
    n_seq, n_res = lax.axis_size("seq"), lax.axis_size("res")
    scale = 1.0 / math.sqrt(embed // H * rows * n_seq)
    flat, half_flat = (rows * sites, embed), (half * sites, embed)
    own = x.reshape(flat)
    cost = 2 * rows * sites * embed * embed

    def part(x, other):
        return call(
            functools.partial(kernel_part, half * sites, other),
            [(half_flat, BF16)],
            (x,),
            scratch=[pltpu.SemaphoreType.DMA],
            space=pltpu.HBM,
        )[0]

    sent_first = part(own, False)
    far_first = swap(sent_first, "res", 2)
    mine, sent_first = lax.optimization_barrier((own, sent_first))
    twin = swap(mine, "res", 1)
    at, total = places(rows, sites, embed)
    (kept,) = call(
        functools.partial(kernel_near, rows, sites, width),
        [((total, embed), BF16)],
        (own, twin, wq, wk, wv),
        6 * cost,
        [pltpu.VMEM(flat, BF16), pltpu.VMEM(flat, BF16), pltpu.SemaphoreType.DMA((5,))],
        pltpu.HBM,
    )
    later, kept = lax.optimization_barrier((own, kept))
    sent_second = part(later, True)
    far_second = swap(sent_second, "res", 2)
    far_first, kept, sent_second = lax.optimization_barrier((far_first, kept, sent_second))
    far_first_twin = swap(far_first, "res", 1)
    sums = ((H * sites, 2 * sites), F32)
    k_far, back = call(
        functools.partial(kernel_back, rows, sites, width),
        [(half_flat, BF16), sums],
        (far_first, kept),
        cost,
        [pltpu.VMEM(half_flat, BF16)],
    )
    far_first_twin, k_far = lax.optimization_barrier((far_first_twin, k_far))
    size = H * sites // GROUP
    part_shape = (size + size // 2, 4 * sites)
    parts = call(
        functools.partial(kernel_ahead, rows, sites, width),
        [(part_shape, F32)] * GROUP,
        (far_first_twin, kept, k_far, back),
        cost,
        [pltpu.VMEM(half_flat, BF16), pltpu.VMEM((H * sites, 4 * sites), F32)],
    )
    came = [swap(parts[k], "seq", k) for k in range(1, GROUP)]
    came[0], kept = lax.optimization_barrier((came[0], kept))
    (v_first,) = call(
        functools.partial(kernel_values, sites, at["wv"]),
        [((half, 2 * sites, embed), BF16)],
        (far_first, far_first_twin, kept),
        cost,
    )
    came[1], v_first = lax.optimization_barrier((came[1], v_first))
    ahead, back = call(
        functools.partial(kernel_sum, size),
        [((size, 4 * sites), F32), ((size // 2, 4 * sites), F32)],
        (parts[0], *came),
    )
    ahead_z = swap(ahead, "seq", GROUP)
    back_x = swap(back, "res", 2)
    cross = [
        (s * n_res + r, (s ^ GROUP) * n_res + (r ^ 2)) for s in range(n_seq) for r in range(n_res)
    ]
    back_xz = lax.ppermute(back, ("seq", "res"), cross)
    (probs,) = call(
        functools.partial(kernel_softmax, scale),
        [((size, 4 * sites), BF16)],
        (ahead, ahead_z, back_x, back_xz),
    )
    far_second, probs = lax.optimization_barrier((far_second, probs))
    far_second_twin = swap(far_second, "res", 1)
    others = [swap(probs, "seq", k) for k in range(1, GROUP)]

    (v_second,) = call(
        functools.partial(kernel_values, sites, at["wv"]),
        [((half, 2 * sites, embed), BF16)],
        (far_second, far_second_twin, kept),
        cost,
    )
    (out,) = call(
        functools.partial(kernel_last, rows, sites, width),
        [(flat, BF16)],
        (probs, *others, kept, v_first, v_second, wo),
        2 * cost,
        [pltpu.VMEM((H * sites, 4 * sites), BF16), pltpu.VMEM(half_flat, BF16)],
    )
    return out.reshape(rows, sites, embed)


def solution(mesh):
    placed = (P("seq", "res", None), P(), P(), P(), P())
    fits = mesh.shape["res"] == 4 and mesh.shape["seq"] == 2 * GROUP
    return jax.shard_map(
        body if fits else plain_body,
        mesh=mesh,
        in_specs=placed,
        out_specs=P("seq", "res", None),
        check_vma=False,
    )
```

```python
import functools
import math

import jax
import jax.numpy as jnp
from jax import lax
from jax.experimental import pallas as pl
from jax.experimental.pallas import tpu as pltpu
from jax.sharding import PartitionSpec as P

H = 12
GROUP = 4
F32, BF16 = jnp.float32, jnp.bfloat16


def reshape_by_group(inputs, weight, attention_groups):
    sequence_number, site_number, embed_size = inputs.shape
    out = jnp.dot(
        inputs.reshape(sequence_number * site_number, embed_size),
        weight,
        preferred_element_type=F32,
    )
    return out.astype(BF16).reshape(
        sequence_number, site_number, attention_groups, embed_size // attention_groups
    )


def plain_body(
    alignment_embedding, probe_projector, lookup_projector, content_projector, final_projector
):
    sequence_number, site_number, embed_size = alignment_embedding.shape
    head_size = embed_size // H
    scale = 1.0 / math.sqrt(head_size * sequence_number * lax.axis_size("seq"))
    probe_tensor = reshape_by_group(alignment_embedding, probe_projector, H)
    gathered = lax.all_gather(alignment_embedding, "res", axis=1, tiled=True)
    all_keys = reshape_by_group(gathered, lookup_projector, H)
    all_values = reshape_by_group(gathered, content_projector, H)
    logits = jnp.einsum("rihe,rjhe->hij", probe_tensor, all_keys, preferred_element_type=F32)
    summed = lax.psum(logits, "seq")
    probs = jax.nn.softmax(summed * scale, axis=-1).astype(BF16)
    attended = jnp.einsum("hij,rjhe->rihe", probs, all_values, preferred_element_type=F32)
    attended = attended.astype(BF16).reshape(sequence_number * site_number, embed_size)
    mixed = jnp.dot(attended, final_projector, preferred_element_type=F32).astype(BF16)
    return mixed.reshape(sequence_number, site_number, embed_size)


def call(kernel, outs, args, flops=0, scratch=(), space=pltpu.VMEM, to=pltpu.VMEM):
    shapes = [jax.ShapeDtypeStruct(s, d) for s, d in outs]
    if space == pltpu.HBM:
        args = [pltpu.with_memory_space_constraint(a, space) for a in args]
    moved = sum(a.size * a.dtype.itemsize for a in list(args) + shapes)
    return pl.pallas_call(
        kernel,
        out_shape=shapes,
        in_specs=[pl.BlockSpec(memory_space=space)] * len(args),
        out_specs=[pl.BlockSpec(memory_space=to)] * len(shapes),
        scratch_shapes=list(scratch),
        cost_estimate=pl.CostEstimate(flops=flops, bytes_accessed=moved, transcendentals=0),
        compiler_params=pltpu.CompilerParams(vmem_limit_bytes=4 * 1024 * 1024),
    )(*args)


def matmul(x, w):
    return jnp.dot(x, w, preferred_element_type=F32).astype(BF16)


def apart(x, sites, store):
    head = x.shape[1] // H
    rows = [x[r : r + sites, :] for r in range(0, x.shape[0], sites)]
    for r in range(0, len(rows), 2):
        for h in range(H):
            lanes = slice(h * head, (h + 1) * head)
            pair = [rows[r][:, lanes], rows[r + 1][:, lanes]]
            store(h, r * head, jnp.concatenate(pair, axis=1))


def keep_apart(x, sites, out, blocks=1, block=0):
    def store(h, lane, pair):
        at = (h * blocks + block) * sites
        out[at : at + sites, lane : lane + pair.shape[1]] = pair

    apart(x, sites, store)


def against(probe, keys):
    return lax.dot_general(probe, keys, (((1,), (1,)), ((), ())), preferred_element_type=F32)


def gray(n):
    return n ^ (n >> 1)


def ring_place():
    me = lax.rem(lax.axis_index("seq"), GROUP)
    return lax.bitwise_xor(me, lax.shift_right_logical(me, 1))


def kernel_part(count, other, x, out, sems):
    place = lax.axis_index("res") // 2
    start = (1 - place if other else place) * count
    piece = count // sems.shape[0]
    copies = [
        pltpu.make_async_copy(
            x.at[pl.ds(start + n * piece, piece)], out.at[pl.ds(n * piece, piece)], sems.at[n]
        )
        for n in range(sems.shape[0])
    ]
    for copy in copies:
        copy.start()
    for copy in copies:
        copy.wait()


def kernel_near(rows, sites, own, twin, wq, wk, wv, kept, q, k, v, near, x_own, x_twin, sems):
    embed = wq.shape[0]
    moves = [(own, x_own), (twin, x_twin)]
    moves += [(w, kept.at[pl.ds(n * embed, embed)]) for n, w in enumerate((wq, wk, wv))]
    own_in, twin_in, wq_in, wk_in, wv_in = copies = [
        pltpu.make_async_copy(source, target, sems.at[n])
        for n, (source, target) in enumerate(moves)
    ]
    for n in (2, 0, 3, 1, 4):
        copies[n].start()
    wq_in.wait()
    own_in.wait()
    keep_apart(matmul(x_own[...], kept[:embed, :]), sites, q)
    wk_in.wait()
    keep_apart(matmul(x_own[...], kept[embed : 2 * embed, :]), sites, k, 2, 0)
    twin_in.wait()
    keep_apart(matmul(x_twin[...], kept[embed : 2 * embed, :]), sites, k, 2, 1)
    for h in range(H):
        mine, both = slice(h * sites, (h + 1) * sites), slice(2 * h * sites, 2 * (h + 1) * sites)
        near[mine, :] = against(q[mine, :], k[both, :])
    wv_in.wait()
    keep_apart(matmul(x_own[...], kept[2 * embed :, :]), sites, v, 2, 0)
    keep_apart(matmul(x_twin[...], kept[2 * embed :, :]), sites, v, 2, 1)


def rows_that_came(half_width):
    came = (1 - lax.axis_index("res") // 2) * half_width
    return pl.ds(pl.multiple_of(came, half_width), half_width)


def kernel_back(sites, x_far, kept, k, k_far, back, q_far):
    embed, came = x_far.shape[1], rows_that_came(k_far.shape[1])
    keep_apart(matmul(x_far[...], kept[:embed, :]), sites, q_far)
    keep_apart(matmul(x_far[...], kept[embed : 2 * embed, :]), sites, k_far)
    for h in range(H):
        mine, both = slice(h * sites, (h + 1) * sites), slice(2 * h * sites, 2 * (h + 1) * sites)
        back[mine, :] = against(q_far[mine, :], k[both, came])


def kernel_ahead(sites, x_far_twin, kept, q, near, k_far, back, *refs):
    parts, (k_twin, ahead) = refs[:GROUP], refs[GROUP:]
    embed, came = x_far_twin.shape[1], rows_that_came(k_far.shape[1])
    me = ring_place()
    keep_apart(matmul(x_far_twin[...], kept[embed : 2 * embed, :]), sites, k_twin)
    for h in range(H):
        mine = slice(h * sites, (h + 1) * sites)
        keys = jnp.concatenate([k_far[mine, :], k_twin[mine, :]], axis=0)
        ahead[mine, :] = jnp.concatenate([near[mine, :], against(q[mine, came], keys)], axis=1)
    size = H * sites // GROUP
    for n in range(GROUP):
        to = lax.rem(me + n, GROUP) * size
        parts[n][:size, :] = ahead[pl.ds(to, size), :]
        parts[n][size:, :] = jnp.concatenate(
            [back[pl.ds(to, size // 2), :], back[pl.ds(to + size // 2, size // 2), :]], axis=1
        )


def kernel_sum(size, a, b, c, d, ahead, back):
    ahead[...] = (a[:size, :] + b[:size, :]) + (c[:size, :] + d[:size, :])
    back[...] = (a[size:, :] + b[size:, :]) + (c[size:, :] + d[size:, :])


def kernel_softmax(scale, ahead, ahead_z, back_x, back_xz, out):
    far = back_x[...] + back_xz[...]
    half = far.shape[1] // 2
    far = jnp.concatenate([far[:, :half], far[:, half:]], axis=0)
    far = jnp.concatenate([jnp.zeros_like(far), far], axis=1)
    logits = (ahead[...] + ahead_z[...] + far) * scale
    e = jnp.exp(logits - jnp.max(logits, axis=1, keepdims=True))
    out[...] = (e / jnp.sum(e, axis=1, keepdims=True)).astype(BF16)


def kernel_values(sites, x, x_twin, kept, out):
    w = kept[2 * x.shape[1] :, :]
    keep_apart(matmul(x[...], w), sites, out, 2, 0)
    keep_apart(matmul(x_twin[...], w), sites, out, 2, 1)


def kernel_last(sites, p0, p1, p2, p3, v_near, v_first, v_second, wo, out, probs, att, mixed, sems):
    place = lax.axis_index("res") // 2
    me = ring_place()
    size, width = H * sites // GROUP, v_first.shape[1]
    head = wo.shape[0] // H
    for n, p in enumerate((p0, p1, p2, p3)):
        probs[pl.ds(lax.rem(me + GROUP - n, GROUP) * size, size), :] = p[...]
    copies = []
    for far, half in ((v_first, 1 - place), (v_second, place)):
        came = pl.ds(pl.multiple_of(half * width, width), width)
        for h in range(0, H, 2):
            pair = []
            for one in (h, h + 1):
                both = slice(2 * one * sites, 2 * (one + 1) * sites)
                v = jnp.concatenate([v_near[both, came], far[both, :]], axis=0)
                p = probs[one * sites : (one + 1) * sites, :]
                pair.append(matmul(p, v))
            for r in range(width // head):
                lanes = slice(r * head, (r + 1) * head)
                att[r * sites : (r + 1) * sites, h * head : (h + 2) * head] = jnp.concatenate(
                    [pair[0][:, lanes], pair[1][:, lanes]], axis=1
                )
        rows = att.shape[0]
        piece = 2 * rows // sems.shape[0]
        for start in range(0, rows, piece):
            n = len(copies)
            mixed[n * piece : (n + 1) * piece, :] = matmul(att[start : start + piece, :], wo[...])
            target = out.at[pl.ds(half * rows + start, piece)]
            copies.append(
                pltpu.make_async_copy(mixed.at[pl.ds(n * piece, piece)], target, sems.at[n])
            )
            copies[n].start()
    for copy in copies:
        copy.wait()


def swap(x, axis, bit):
    count = lax.axis_size(axis)
    return lax.ppermute(x, axis, [(i, i ^ bit) for i in range(count)])


def turn(x, steps):
    count = lax.axis_size("seq")
    to = [s // GROUP * GROUP + gray((gray(s % GROUP) + steps) % GROUP) for s in range(count)]
    return lax.ppermute(x, "seq", list(enumerate(to)))


def body(x, wq, wk, wv, wo):
    rows, sites, embed = x.shape
    half, head = rows // 2, embed // H
    n_seq, n_res = lax.axis_size("seq"), lax.axis_size("res")
    scale = 1.0 / math.sqrt(head * rows * n_seq)
    flat, half_flat = (rows * sites, embed), (half * sites, embed)
    own = x.reshape(flat)
    cost = 2 * rows * sites * embed * embed

    def part(x, other):
        return call(
            functools.partial(kernel_part, half * sites, other),
            [(half_flat, BF16)],
            (x,),
            scratch=[pltpu.SemaphoreType.DMA((GROUP,))],
            space=pltpu.HBM,
        )[0]

    sent_first = part(own, False)
    far_first = swap(sent_first, "res", 2)
    mine, sent_first = lax.optimization_barrier((own, sent_first))
    twin = swap(mine, "res", 1)
    sums = ((H * sites, 2 * sites), F32)

    def heads(blocks, count):
        return ((H * blocks * sites, count * head), BF16)

    kept, q, k, v_near, near = call(
        functools.partial(kernel_near, rows, sites),
        [((3 * embed, embed), BF16), heads(1, rows), heads(2, rows), heads(2, rows), sums],
        (own, twin, wq, wk, wv),
        6 * cost,
        [pltpu.VMEM(flat, BF16), pltpu.VMEM(flat, BF16), pltpu.SemaphoreType.DMA((5,))],
        pltpu.HBM,
    )
    later, kept = lax.optimization_barrier((own, kept))
    sent_second = part(later, True)
    far_second = swap(sent_second, "res", 2)
    far_first, kept, sent_second = lax.optimization_barrier((far_first, kept, sent_second))
    far_first_twin = swap(far_first, "res", 1)
    k_far, back = call(
        functools.partial(kernel_back, sites),
        [heads(1, half), sums],
        (far_first, kept, k),
        cost,
        [pltpu.VMEM(*heads(1, half))],
    )
    far_first_twin, k_far = lax.optimization_barrier((far_first_twin, k_far))
    size = H * sites // GROUP
    part_shape = (size + size // 2, 4 * sites)
    parts = call(
        functools.partial(kernel_ahead, sites),
        [(part_shape, F32)] * GROUP,
        (far_first_twin, kept, q, near, k_far, back),
        cost,
        [pltpu.VMEM(*heads(1, half)), pltpu.VMEM((H * sites, 4 * sites), F32)],
    )
    came = [turn(parts[k], k) for k in range(1, GROUP)]
    came[0], kept = lax.optimization_barrier((came[0], kept))
    (v_first,) = call(
        functools.partial(kernel_values, sites),
        [heads(2, half)],
        (far_first, far_first_twin, kept),
        cost,
    )
    came[1], v_first = lax.optimization_barrier((came[1], v_first))
    ahead, back = call(
        functools.partial(kernel_sum, size),
        [((size, 4 * sites), F32), ((size // 2, 4 * sites), F32)],
        (parts[0], *came),
    )
    ahead_z = swap(ahead, "seq", GROUP)
    back_x = swap(back, "res", 2)
    cross = [
        (s * n_res + r, (s ^ GROUP) * n_res + (r ^ 2)) for s in range(n_seq) for r in range(n_res)
    ]
    back_xz = lax.ppermute(back, ("seq", "res"), cross)
    (probs,) = call(
        functools.partial(kernel_softmax, scale),
        [((size, 4 * sites), BF16)],
        (ahead, ahead_z, back_x, back_xz),
    )
    far_second, probs = lax.optimization_barrier((far_second, probs))
    far_second_twin = swap(far_second, "res", 1)
    others = [turn(probs, k) for k in range(1, GROUP)]

    (v_second,) = call(
        functools.partial(kernel_values, sites),
        [heads(2, half)],
        (far_second, far_second_twin, kept),
        cost,
    )
    (out,) = call(
        functools.partial(kernel_last, sites),
        [(flat, BF16)],
        (probs, *others, v_near, v_first, v_second, wo),
        2 * cost,
        [
            pltpu.VMEM((H * sites, 4 * sites), BF16),
            pltpu.VMEM(half_flat, BF16),
            pltpu.VMEM(flat, BF16),
            pltpu.SemaphoreType.DMA((4,)),
        ],
        to=pltpu.HBM,
    )
    return out.reshape(rows, sites, embed)


def solution(mesh):
    placed = (P("seq", "res", None), P(), P(), P(), P())
    fits = mesh.shape["res"] == 4 and mesh.shape["seq"] == 2 * GROUP
    return jax.shard_map(
        body if fits else plain_body,
        mesh=mesh,
        in_specs=placed,
        out_specs=P("seq", "res", None),
        check_vma=False,
    )
```

```python
import functools
import math

import jax
import jax.numpy as jnp
from jax import lax
from jax.experimental import pallas as pl
from jax.experimental.pallas import tpu as pltpu
from jax.sharding import PartitionSpec as P

H = 12
GROUP = 4
F32, BF16 = jnp.float32, jnp.bfloat16


def reshape_by_group(inputs, weight, attention_groups):
    sequence_number, site_number, embed_size = inputs.shape
    out = jnp.dot(
        inputs.reshape(sequence_number * site_number, embed_size),
        weight,
        preferred_element_type=F32,
    )
    return out.astype(BF16).reshape(
        sequence_number, site_number, attention_groups, embed_size // attention_groups
    )


def plain_body(
    alignment_embedding, probe_projector, lookup_projector, content_projector, final_projector
):
    sequence_number, site_number, embed_size = alignment_embedding.shape
    head_size = embed_size // H
    scale = 1.0 / math.sqrt(head_size * sequence_number * lax.axis_size("seq"))
    probe_tensor = reshape_by_group(alignment_embedding, probe_projector, H)
    gathered = lax.all_gather(alignment_embedding, "res", axis=1, tiled=True)
    all_keys = reshape_by_group(gathered, lookup_projector, H)
    all_values = reshape_by_group(gathered, content_projector, H)
    logits = jnp.einsum("rihe,rjhe->hij", probe_tensor, all_keys, preferred_element_type=F32)
    summed = lax.psum(logits, "seq")
    probs = jax.nn.softmax(summed * scale, axis=-1).astype(BF16)
    attended = jnp.einsum("hij,rjhe->rihe", probs, all_values, preferred_element_type=F32)
    attended = attended.astype(BF16).reshape(sequence_number * site_number, embed_size)
    mixed = jnp.dot(attended, final_projector, preferred_element_type=F32).astype(BF16)
    return mixed.reshape(sequence_number, site_number, embed_size)


def call(kernel, outs, args, flops=0, scratch=(), space=pltpu.VMEM, to=pltpu.VMEM):
    shapes = [jax.ShapeDtypeStruct(s, d) for s, d in outs]
    if space == pltpu.HBM:
        args = [pltpu.with_memory_space_constraint(a, space) for a in args]
    moved = sum(a.size * a.dtype.itemsize for a in list(args) + shapes)
    return pl.pallas_call(
        kernel,
        out_shape=shapes,
        in_specs=[pl.BlockSpec(memory_space=space)] * len(args),
        out_specs=[pl.BlockSpec(memory_space=to)] * len(shapes),
        scratch_shapes=list(scratch),
        cost_estimate=pl.CostEstimate(flops=flops, bytes_accessed=moved, transcendentals=0),
        compiler_params=pltpu.CompilerParams(vmem_limit_bytes=4 * 1024 * 1024),
    )(*args)


def matmul(x, w):
    return jnp.dot(x, w, preferred_element_type=F32).astype(BF16)


def apart(x, sites, store):
    head = x.shape[1] // H
    rows = [x[r : r + sites, :] for r in range(0, x.shape[0], sites)]
    for r in range(0, len(rows), 2):
        for h in range(H):
            lanes = slice(h * head, (h + 1) * head)
            pair = [rows[r][:, lanes], rows[r + 1][:, lanes]]
            store(h, r * head, jnp.concatenate(pair, axis=1))


def keep_apart(x, sites, out, blocks=1, block=0):
    def store(h, lane, pair):
        at = (h * blocks + block) * sites
        out[at : at + sites, lane : lane + pair.shape[1]] = pair

    apart(x, sites, store)


def against(probe, keys):
    return lax.dot_general(probe, keys, (((1,), (1,)), ((), ())), preferred_element_type=F32)


def gray(n):
    return n ^ (n >> 1)


def ring_place(other=0):
    place = lax.bitwise_xor(lax.rem(lax.axis_index("seq"), GROUP), other)
    return lax.bitwise_xor(place, lax.shift_right_logical(place, 1))


def kernel_part(count, other, x, out, sems):
    place = lax.axis_index("res") // 2
    start = (1 - place if other else place) * count
    piece = count // sems.shape[0]
    copies = [
        pltpu.make_async_copy(
            x.at[pl.ds(start + n * piece, piece)], out.at[pl.ds(n * piece, piece)], sems.at[n]
        )
        for n in range(sems.shape[0])
    ]
    for copy in copies:
        copy.start()
    for copy in copies:
        copy.wait()


def kernel_near(rows, sites, own, twin, wq, wk, wv, kept, q, k, v, near, x_own, x_twin, sems):
    embed = wq.shape[0]
    moves = [(own, x_own), (twin, x_twin)]
    moves += [(w, kept.at[pl.ds(n * embed, embed)]) for n, w in enumerate((wq, wk, wv))]
    own_in, twin_in, wq_in, wk_in, wv_in = copies = [
        pltpu.make_async_copy(source, target, sems.at[n])
        for n, (source, target) in enumerate(moves)
    ]
    for n in (2, 0, 3, 1, 4):
        copies[n].start()
    wq_in.wait()
    own_in.wait()
    keep_apart(matmul(x_own[...], kept[:embed, :]), sites, q)
    wk_in.wait()
    keep_apart(matmul(x_own[...], kept[embed : 2 * embed, :]), sites, k, 2, 0)
    twin_in.wait()
    keep_apart(matmul(x_twin[...], kept[embed : 2 * embed, :]), sites, k, 2, 1)
    for h in range(H):
        mine, both = slice(h * sites, (h + 1) * sites), slice(2 * h * sites, 2 * (h + 1) * sites)
        near[mine, :] = against(q[mine, :], k[both, :])
    wv_in.wait()
    keep_apart(matmul(x_own[...], kept[2 * embed :, :]), sites, v, 2, 0)
    keep_apart(matmul(x_twin[...], kept[2 * embed :, :]), sites, v, 2, 1)


def rows_that_came(half_width):
    came = (1 - lax.axis_index("res") // 2) * half_width
    return pl.ds(pl.multiple_of(came, half_width), half_width)


def kernel_back(sites, x_far, kept, k, k_far, back, q_far, total):
    embed, came = x_far.shape[1], rows_that_came(k_far.shape[1])
    keep_apart(matmul(x_far[...], kept[:embed, :]), sites, q_far)
    keep_apart(matmul(x_far[...], kept[embed : 2 * embed, :]), sites, k_far)
    for h in range(H):
        mine, both = slice(h * sites, (h + 1) * sites), slice(2 * h * sites, 2 * (h + 1) * sites)
        total[mine, :] = against(q_far[mine, :], k[both, came])
    half = total.shape[0] // 2
    back[...] = jnp.concatenate([total[:half, :], total[half:, :]], axis=1)


def kernel_ahead(sites, x_far_twin, kept, q, k_far, ahead, k_twin):
    embed, came = x_far_twin.shape[1], rows_that_came(k_far.shape[1])
    keep_apart(matmul(x_far_twin[...], kept[embed : 2 * embed, :]), sites, k_twin)
    for h in range(H):
        mine = slice(h * sites, (h + 1) * sites)
        keys = jnp.concatenate([k_far[mine, :], k_twin[mine, :]], axis=0)
        ahead[mine, :] = against(q[mine, came], keys)


def kernel_mix(near, ahead, back, *refs):
    *parts, total = refs
    half = near.shape[0] // 2
    for rows, lanes in (
        (slice(0, half), slice(0, near.shape[1])),
        (slice(half, 2 * half), slice(near.shape[1], 2 * near.shape[1])),
    ):
        far = ahead[rows, :] + back[:, lanes]
        total[rows, :] = jnp.concatenate([near[rows, :], far], axis=1)
    me, size = ring_place(), total.shape[0] // GROUP
    for n, part in enumerate(parts):
        part[...] = total[pl.ds(lax.rem(me + n, GROUP) * size, size), :]


def kernel_sum(a, b, c, d, out):
    out[...] = (a[...] + b[...]) + (c[...] + d[...])


def kernel_softmax(scale, mine, other, out):
    logits = (mine[...] + other[...]) * scale
    e = jnp.exp(logits - jnp.max(logits, axis=1, keepdims=True))
    out[...] = (e / jnp.sum(e, axis=1, keepdims=True)).astype(BF16)


def kernel_values(sites, x, x_twin, kept, out):
    w = kept[2 * x.shape[1] :, :]
    keep_apart(matmul(x[...], w), sites, out, 2, 0)
    keep_apart(matmul(x_twin[...], w), sites, out, 2, 1)


def kernel_last(sites, p0, p1, p2, p3, v_near, v_first, v_second, wo, out, probs, att, mixed, sems):
    place = lax.axis_index("res") // 2
    size, width = H * sites // GROUP, v_first.shape[1]
    head = wo.shape[0] // H
    for n, p in enumerate((p0, p1, p2, p3)):
        probs[pl.ds(ring_place(n) * size, size), :] = p[...]
    copies = []
    for far, half in ((v_first, 1 - place), (v_second, place)):
        came = pl.ds(pl.multiple_of(half * width, width), width)
        for h in range(0, H, 2):
            pair = []
            for one in (h, h + 1):
                both = slice(2 * one * sites, 2 * (one + 1) * sites)
                v = jnp.concatenate([v_near[both, came], far[both, :]], axis=0)
                p = probs[one * sites : (one + 1) * sites, :]
                pair.append(matmul(p, v))
            for r in range(width // head):
                lanes = slice(r * head, (r + 1) * head)
                att[r * sites : (r + 1) * sites, h * head : (h + 2) * head] = jnp.concatenate(
                    [pair[0][:, lanes], pair[1][:, lanes]], axis=1
                )
        rows = att.shape[0]
        piece = 2 * rows // sems.shape[0]
        for start in range(0, rows, piece):
            n = len(copies)
            mixed[n * piece : (n + 1) * piece, :] = matmul(att[start : start + piece, :], wo[...])
            target = out.at[pl.ds(half * rows + start, piece)]
            copies.append(
                pltpu.make_async_copy(mixed.at[pl.ds(n * piece, piece)], target, sems.at[n])
            )
            copies[n].start()
    for copy in copies:
        copy.wait()


def swap(x, axis, bit):
    count = lax.axis_size(axis)
    return lax.ppermute(x, axis, [(i, i ^ bit) for i in range(count)])


def turn(x, steps):
    count = lax.axis_size("seq")
    to = [s // GROUP * GROUP + gray((gray(s % GROUP) + steps) % GROUP) for s in range(count)]
    return lax.ppermute(x, "seq", list(enumerate(to)))


def body(x, wq, wk, wv, wo):
    rows, sites, embed = x.shape
    half, head = rows // 2, embed // H
    n_seq = lax.axis_size("seq")
    scale = 1.0 / math.sqrt(head * rows * n_seq)
    flat, half_flat = (rows * sites, embed), (half * sites, embed)
    own = x.reshape(flat)
    cost = 2 * rows * sites * embed * embed

    def part(x, other):
        return call(
            functools.partial(kernel_part, half * sites, other),
            [(half_flat, BF16)],
            (x,),
            scratch=[pltpu.SemaphoreType.DMA((GROUP,))],
            space=pltpu.HBM,
        )[0]

    sent_first = part(own, False)
    far_first = swap(sent_first, "res", 2)
    mine, sent_first = lax.optimization_barrier((own, sent_first))
    twin = swap(mine, "res", 1)
    sums = ((H * sites, 2 * sites), F32)

    def heads(blocks, count):
        return ((H * blocks * sites, count * head), BF16)

    size = H * sites // GROUP
    share = ((size, 4 * sites), F32)
    kept, q, k, v_near, near = call(
        functools.partial(kernel_near, rows, sites),
        [((3 * embed, embed), BF16), heads(1, rows), heads(2, rows), heads(2, rows), sums],
        (own, twin, wq, wk, wv),
        6 * cost,
        [pltpu.VMEM(flat, BF16), pltpu.VMEM(flat, BF16), pltpu.SemaphoreType.DMA((5,))],
        pltpu.HBM,
    )
    later, kept = lax.optimization_barrier((own, kept))
    sent_second = part(later, True)
    far_first, kept, sent_second = lax.optimization_barrier((far_first, kept, sent_second))
    far_first_twin = swap(far_first, "res", 1)
    k_far, back = call(
        functools.partial(kernel_back, sites),
        [heads(1, half), ((H * sites // 2, 4 * sites), F32)],
        (far_first, kept, k),
        cost,
        [pltpu.VMEM(*heads(1, half)), pltpu.VMEM(*sums)],
    )
    back = swap(back, "res", 2)
    far_first_twin, k_far, sent_second = lax.optimization_barrier(
        (far_first_twin, k_far, sent_second)
    )
    far_second = swap(sent_second, "res", 2)
    (ahead,) = call(
        functools.partial(kernel_ahead, sites),
        [sums],
        (far_first_twin, kept, q, k_far),
        cost,
        [pltpu.VMEM(*heads(1, half))],
    )
    wide = ((H * sites, 4 * sites), F32)
    far = call(kernel_mix, [share] * GROUP, (near, ahead, back), 0, [pltpu.VMEM(*wide)])
    far = [far[0]] + [turn(far[n], n) for n in range(1, GROUP)]
    far[1], kept = lax.optimization_barrier((far[1], kept))
    (v_first,) = call(
        functools.partial(kernel_values, sites),
        [heads(2, half)],
        (far_first, far_first_twin, kept),
        cost,
    )
    far[2], v_first = lax.optimization_barrier((far[2], v_first))
    (mine,) = call(kernel_sum, [share], far)
    (probs,) = call(
        functools.partial(kernel_softmax, scale),
        [((size, 4 * sites), BF16)],
        (mine, swap(mine, "seq", GROUP)),
        2000000000,
    )
    far_second, probs = lax.optimization_barrier((far_second, probs))
    far_second_twin = swap(far_second, "res", 1)
    others = [swap(probs, "seq", k) for k in range(1, GROUP)]

    (v_second,) = call(
        functools.partial(kernel_values, sites),
        [heads(2, half)],
        (far_second, far_second_twin, kept),
        cost,
    )
    (out,) = call(
        functools.partial(kernel_last, sites),
        [(flat, BF16)],
        (probs, *others, v_near, v_first, v_second, wo),
        2 * cost,
        [
            pltpu.VMEM((H * sites, 4 * sites), BF16),
            pltpu.VMEM(half_flat, BF16),
            pltpu.VMEM(flat, BF16),
            pltpu.SemaphoreType.DMA((4,)),
        ],
        to=pltpu.HBM,
    )
    return out.reshape(rows, sites, embed)


def solution(mesh):
    placed = (P("seq", "res", None), P(), P(), P(), P())
    fits = mesh.shape["res"] == 4 and mesh.shape["seq"] == 2 * GROUP
    return jax.shard_map(
        body if fits else plain_body,
        mesh=mesh,
        in_specs=placed,
        out_specs=P("seq", "res", None),
        check_vma=False,
    )
```

```python
import functools
import math

import jax
import jax.numpy as jnp
from jax import lax
from jax.experimental import pallas as pl
from jax.experimental.pallas import tpu as pltpu
from jax.sharding import PartitionSpec as P

H = 12
GROUP = 4
F32, BF16 = jnp.float32, jnp.bfloat16


def reshape_by_group(inputs, weight, attention_groups):
    sequence_number, site_number, embed_size = inputs.shape
    out = jnp.dot(
        inputs.reshape(sequence_number * site_number, embed_size),
        weight,
        preferred_element_type=F32,
    )
    return out.astype(BF16).reshape(
        sequence_number, site_number, attention_groups, embed_size // attention_groups
    )


def plain_body(
    alignment_embedding, probe_projector, lookup_projector, content_projector, final_projector
):
    sequence_number, site_number, embed_size = alignment_embedding.shape
    head_size = embed_size // H
    scale = 1.0 / math.sqrt(head_size * sequence_number * lax.axis_size("seq"))
    probe_tensor = reshape_by_group(alignment_embedding, probe_projector, H)
    gathered = lax.all_gather(alignment_embedding, "res", axis=1, tiled=True)
    all_keys = reshape_by_group(gathered, lookup_projector, H)
    all_values = reshape_by_group(gathered, content_projector, H)
    logits = jnp.einsum("rihe,rjhe->hij", probe_tensor, all_keys, preferred_element_type=F32)
    summed = lax.psum(logits, "seq")
    probs = jax.nn.softmax(summed * scale, axis=-1).astype(BF16)
    attended = jnp.einsum("hij,rjhe->rihe", probs, all_values, preferred_element_type=F32)
    attended = attended.astype(BF16).reshape(sequence_number * site_number, embed_size)
    mixed = jnp.dot(attended, final_projector, preferred_element_type=F32).astype(BF16)
    return mixed.reshape(sequence_number, site_number, embed_size)


def call(kernel, outs, args, flops=0, scratch=(), space=pltpu.VMEM, to=pltpu.VMEM):
    shapes = [jax.ShapeDtypeStruct(s, d) for s, d in outs]
    if space == pltpu.HBM:
        args = [pltpu.with_memory_space_constraint(a, space) for a in args]
    moved = sum(a.size * a.dtype.itemsize for a in list(args) + shapes)
    return pl.pallas_call(
        kernel,
        out_shape=shapes,
        in_specs=[pl.BlockSpec(memory_space=space)] * len(args),
        out_specs=[pl.BlockSpec(memory_space=to)] * len(shapes),
        scratch_shapes=list(scratch),
        cost_estimate=pl.CostEstimate(flops=flops, bytes_accessed=moved, transcendentals=0),
        compiler_params=pltpu.CompilerParams(vmem_limit_bytes=4 * 1024 * 1024),
    )(*args)


def matmul(x, w):
    return jnp.dot(x, w, preferred_element_type=F32).astype(BF16)


def apart(x, sites, store):
    head = x.shape[1] // H
    rows = [x[r : r + sites, :] for r in range(0, x.shape[0], sites)]
    for r in range(0, len(rows), 2):
        for h in range(H):
            lanes = slice(h * head, (h + 1) * head)
            pair = [rows[r][:, lanes], rows[r + 1][:, lanes]]
            store(h, r * head, jnp.concatenate(pair, axis=1))


def keep_apart(x, sites, out, blocks=1, block=0):
    def store(h, lane, pair):
        at = (h * blocks + block) * sites
        out[at : at + sites, lane : lane + pair.shape[1]] = pair

    apart(x, sites, store)


def against(probe, keys):
    return lax.dot_general(probe, keys, (((1,), (1,)), ((), ())), preferred_element_type=F32)


def gray(n):
    return n ^ (n >> 1)


def ring_place(other=0):
    place = lax.bitwise_xor(lax.rem(lax.axis_index("seq"), GROUP), other)
    return lax.bitwise_xor(place, lax.shift_right_logical(place, 1))


def kernel_part(count, other, x, out, sems):
    place = lax.axis_index("res") // 2
    start = (1 - place if other else place) * count
    piece = count // sems.shape[0]
    copies = [
        pltpu.make_async_copy(
            x.at[pl.ds(start + n * piece, piece)], out.at[pl.ds(n * piece, piece)], sems.at[n]
        )
        for n in range(sems.shape[0])
    ]
    for copy in copies:
        copy.start()
    for copy in copies:
        copy.wait()


def kernel_near(rows, sites, own, twin, wq, wk, wv, kept, q, k, v, near, x_own, x_twin, sems):
    embed = wq.shape[0]
    moves = [(own, x_own), (twin, x_twin)]
    moves += [(w, kept.at[pl.ds(n * embed, embed)]) for n, w in enumerate((wq, wk, wv))]
    own_in, twin_in, wq_in, wk_in, wv_in = copies = [
        pltpu.make_async_copy(source, target, sems.at[n])
        for n, (source, target) in enumerate(moves)
    ]
    for n in (2, 0, 3, 1, 4):
        copies[n].start()
    wq_in.wait()
    own_in.wait()
    keep_apart(matmul(x_own[...], kept[:embed, :]), sites, q)
    wk_in.wait()
    keep_apart(matmul(x_own[...], kept[embed : 2 * embed, :]), sites, k, 2, 0)
    twin_in.wait()
    keep_apart(matmul(x_twin[...], kept[embed : 2 * embed, :]), sites, k, 2, 1)
    for h in range(H):
        mine, both = slice(h * sites, (h + 1) * sites), slice(2 * h * sites, 2 * (h + 1) * sites)
        near[mine, :] = against(q[mine, :], k[both, :])
    wv_in.wait()
    keep_apart(matmul(x_own[...], kept[2 * embed :, :]), sites, v, 2, 0)
    keep_apart(matmul(x_twin[...], kept[2 * embed :, :]), sites, v, 2, 1)


def rows_that_came(half_width):
    came = (1 - lax.axis_index("res") // 2) * half_width
    return pl.ds(pl.multiple_of(came, half_width), half_width)


def kernel_back(sites, x_far, kept, k, back, q_far, total):
    embed, came = x_far.shape[1], rows_that_came(q_far.shape[1])
    keep_apart(matmul(x_far[...], kept[:embed, :]), sites, q_far)
    for h in range(H):
        mine, both = slice(h * sites, (h + 1) * sites), slice(2 * h * sites, 2 * (h + 1) * sites)
        total[mine, :] = against(q_far[mine, :], k[both, came])
    half = total.shape[0] // 2
    back[...] = jnp.concatenate([total[:half, :], total[half:, :]], axis=1)


def kernel_ahead(sites, x_far, x_far_twin, kept, q, ahead, k_far, k_twin):
    embed, came = x_far_twin.shape[1], rows_that_came(k_far.shape[1])
    keep_apart(matmul(x_far[...], kept[embed : 2 * embed, :]), sites, k_far)
    keep_apart(matmul(x_far_twin[...], kept[embed : 2 * embed, :]), sites, k_twin)
    for h in range(H):
        mine = slice(h * sites, (h + 1) * sites)
        keys = jnp.concatenate([k_far[mine, :], k_twin[mine, :]], axis=0)
        ahead[mine, :] = against(q[mine, came], keys)


def kernel_mix(near, ahead, back, *refs):
    *parts, total = refs
    half = near.shape[0] // 2
    for rows, lanes in (
        (slice(0, half), slice(0, near.shape[1])),
        (slice(half, 2 * half), slice(near.shape[1], 2 * near.shape[1])),
    ):
        far = ahead[rows, :] + back[:, lanes]
        total[rows, :] = jnp.concatenate([near[rows, :], far], axis=1)
    me, size = ring_place(), total.shape[0] // GROUP
    for n, part in enumerate(parts):
        part[...] = total[pl.ds(lax.rem(me + n, GROUP) * size, size), :]


def kernel_sum(a, b, c, d, out):
    out[...] = (a[...] + b[...]) + (c[...] + d[...])


def kernel_softmax(scale, mine, other, out):
    logits = (mine[...] + other[...]) * scale
    e = jnp.exp(logits - jnp.max(logits, axis=1, keepdims=True))
    out[...] = (e / jnp.sum(e, axis=1, keepdims=True)).astype(BF16)


def kernel_values(sites, x, x_twin, kept, out):
    w = kept[2 * x.shape[1] :, :]
    keep_apart(matmul(x[...], w), sites, out, 2, 0)
    keep_apart(matmul(x_twin[...], w), sites, out, 2, 1)


def kernel_last(sites, p0, p1, p2, p3, v_near, v_first, v_second, wo, out, probs, att, mixed, sems):
    place = lax.axis_index("res") // 2
    size, width = H * sites // GROUP, v_first.shape[1]
    head = wo.shape[0] // H
    for n, p in enumerate((p0, p1, p2, p3)):
        probs[pl.ds(ring_place(n) * size, size), :] = p[...]
    rows, halves = out.shape[0] // 2, (1 - place, place)
    for n, far in enumerate((v_first, v_second)):
        came = pl.ds(pl.multiple_of(halves[n] * width, width), width)
        for h in range(0, H, 2):
            pair = []
            for one in (h, h + 1):
                both = slice(2 * one * sites, 2 * (one + 1) * sites)
                v = jnp.concatenate([v_near[both, came], far[both, :]], axis=0)
                p = probs[one * sites : (one + 1) * sites, :]
                pair.append(matmul(p, v))
            for r in range(width // head):
                lanes, to = slice(r * head, (r + 1) * head), n * rows + r * sites
                att[to : to + sites, h * head : (h + 2) * head] = jnp.concatenate(
                    [pair[0][:, lanes], pair[1][:, lanes]], axis=1
                )
    copies = []
    piece = 2 * wo.shape[1] // sems.shape[0]
    for start in range(0, wo.shape[1], piece):
        lanes = slice(start, start + piece)
        mixed[:, lanes] = matmul(att[...], wo[:, lanes])
        for n, half in enumerate(halves):
            source = mixed.at[n * rows : (n + 1) * rows, lanes]
            target = out.at[pl.ds(half * rows, rows), lanes]
            copies.append(pltpu.make_async_copy(source, target, sems.at[len(copies)]))
            copies[-1].start()
    for copy in copies:
        copy.wait()


def swap(x, axis, bit):
    count = lax.axis_size(axis)
    return lax.ppermute(x, axis, [(i, i ^ bit) for i in range(count)])


def turn(x, steps):
    count = lax.axis_size("seq")
    to = [s // GROUP * GROUP + gray((gray(s % GROUP) + steps) % GROUP) for s in range(count)]
    return lax.ppermute(x, "seq", list(enumerate(to)))


def body(x, wq, wk, wv, wo):
    rows, sites, embed = x.shape
    half, head = rows // 2, embed // H
    n_seq = lax.axis_size("seq")
    scale = 1.0 / math.sqrt(head * rows * n_seq)
    flat, half_flat = (rows * sites, embed), (half * sites, embed)
    own = x.reshape(flat)
    cost = 2 * rows * sites * embed * embed

    def part(x, other):
        return call(
            functools.partial(kernel_part, half * sites, other),
            [(half_flat, BF16)],
            (x,),
            scratch=[pltpu.SemaphoreType.DMA((GROUP,))],
            space=pltpu.HBM,
        )[0]

    sent_first = part(own, False)
    far_first = swap(sent_first, "res", 2)
    mine, sent_first = lax.optimization_barrier((own, sent_first))
    twin = swap(mine, "res", 1)
    sums = ((H * sites, 2 * sites), F32)

    def heads(blocks, count):
        return ((H * blocks * sites, count * head), BF16)

    size = H * sites // GROUP
    share = ((size, 4 * sites), F32)
    kept, q, k, v_near, near = call(
        functools.partial(kernel_near, rows, sites),
        [((3 * embed, embed), BF16), heads(1, rows), heads(2, rows), heads(2, rows), sums],
        (own, twin, wq, wk, wv),
        6 * cost,
        [pltpu.VMEM(flat, BF16), pltpu.VMEM(flat, BF16), pltpu.SemaphoreType.DMA((5,))],
        pltpu.HBM,
    )
    later, kept = lax.optimization_barrier((own, kept))
    sent_second = part(later, True)
    far_first, kept, sent_second = lax.optimization_barrier((far_first, kept, sent_second))
    far_first_twin = swap(far_first, "res", 1)
    (sent_back,) = call(
        functools.partial(kernel_back, sites),
        [((H * sites // 2, 4 * sites), F32)],
        (far_first, kept, k),
        cost,
        [pltpu.VMEM(*heads(1, half)), pltpu.VMEM(*sums)],
    )
    back = swap(sent_back, "res", 2)
    far_first_twin, sent_back, sent_second = lax.optimization_barrier(
        (far_first_twin, sent_back, sent_second)
    )
    far_second = swap(sent_second, "res", 2)
    (ahead,) = call(
        functools.partial(kernel_ahead, sites),
        [sums],
        (far_first, far_first_twin, kept, q),
        cost,
        [pltpu.VMEM(*heads(1, half)), pltpu.VMEM(*heads(1, half))],
    )
    wide = ((H * sites, 4 * sites), F32)
    far = call(kernel_mix, [share] * GROUP, (near, ahead, back), 0, [pltpu.VMEM(*wide)])
    far = [far[0]] + [turn(far[n], n) for n in range(1, GROUP)]
    far[1], kept = lax.optimization_barrier((far[1], kept))
    (v_first,) = call(
        functools.partial(kernel_values, sites),
        [heads(2, half)],
        (far_first, far_first_twin, kept),
        cost,
    )
    far[2], v_first = lax.optimization_barrier((far[2], v_first))
    (mine,) = call(kernel_sum, [share], far)
    (probs,) = call(
        functools.partial(kernel_softmax, scale),
        [((size, 4 * sites), BF16)],
        (mine, swap(mine, "seq", GROUP)),
        2000000000,
    )
    far_second, probs = lax.optimization_barrier((far_second, probs))
    far_second_twin = swap(far_second, "res", 1)
    others = [swap(probs, "seq", k) for k in range(1, GROUP)]

    (v_second,) = call(
        functools.partial(kernel_values, sites),
        [heads(2, half)],
        (far_second, far_second_twin, kept),
        cost,
    )
    (out,) = call(
        functools.partial(kernel_last, sites),
        [(flat, BF16)],
        (probs, *others, v_near, v_first, v_second, wo),
        2 * cost,
        [
            pltpu.VMEM((H * sites, 4 * sites), BF16),
            pltpu.VMEM(flat, BF16),
            pltpu.VMEM(flat, BF16),
            pltpu.SemaphoreType.DMA((2 * H // GROUP,)),
        ],
        to=pltpu.HBM,
    )
    return out.reshape(rows, sites, embed)


def solution(mesh):
    placed = (P("seq", "res", None), P(), P(), P(), P())
    fits = mesh.shape["res"] == 4 and mesh.shape["seq"] == 2 * GROUP
    return jax.shard_map(
        body if fits else plain_body,
        mesh=mesh,
        in_specs=placed,
        out_specs=P("seq", "res", None),
        check_vma=False,
    )
```

```python
import functools
import math

import jax
import jax.numpy as jnp
from jax import lax
from jax.experimental import pallas as pl
from jax.experimental.pallas import tpu as pltpu
from jax.sharding import PartitionSpec as P

H = 12
GROUP = 4
F32, BF16 = jnp.float32, jnp.bfloat16


def reshape_by_group(inputs, weight, attention_groups):
    sequence_number, site_number, embed_size = inputs.shape
    out = jnp.dot(
        inputs.reshape(sequence_number * site_number, embed_size),
        weight,
        preferred_element_type=F32,
    )
    return out.astype(BF16).reshape(
        sequence_number, site_number, attention_groups, embed_size // attention_groups
    )


def plain_body(
    alignment_embedding, probe_projector, lookup_projector, content_projector, final_projector
):
    sequence_number, site_number, embed_size = alignment_embedding.shape
    head_size = embed_size // H
    scale = 1.0 / math.sqrt(head_size * sequence_number * lax.axis_size("seq"))
    probe_tensor = reshape_by_group(alignment_embedding, probe_projector, H)
    gathered = lax.all_gather(alignment_embedding, "res", axis=1, tiled=True)
    all_keys = reshape_by_group(gathered, lookup_projector, H)
    all_values = reshape_by_group(gathered, content_projector, H)
    logits = jnp.einsum("rihe,rjhe->hij", probe_tensor, all_keys, preferred_element_type=F32)
    summed = lax.psum(logits, "seq")
    probs = jax.nn.softmax(summed * scale, axis=-1).astype(BF16)
    attended = jnp.einsum("hij,rjhe->rihe", probs, all_values, preferred_element_type=F32)
    attended = attended.astype(BF16).reshape(sequence_number * site_number, embed_size)
    mixed = jnp.dot(attended, final_projector, preferred_element_type=F32).astype(BF16)
    return mixed.reshape(sequence_number, site_number, embed_size)


def call(kernel, outs, args, flops=0, scratch=(), space=pltpu.VMEM, to=pltpu.VMEM):
    shapes = [jax.ShapeDtypeStruct(s, d) for s, d in outs]
    if space == pltpu.HBM:
        args = [pltpu.with_memory_space_constraint(a, space) for a in args]
    moved = sum(a.size * a.dtype.itemsize for a in list(args) + shapes)
    return pl.pallas_call(
        kernel,
        out_shape=shapes,
        in_specs=[pl.BlockSpec(memory_space=space)] * len(args),
        out_specs=[pl.BlockSpec(memory_space=to)] * len(shapes),
        scratch_shapes=list(scratch),
        cost_estimate=pl.CostEstimate(flops=flops, bytes_accessed=moved, transcendentals=0),
        compiler_params=pltpu.CompilerParams(vmem_limit_bytes=4 * 1024 * 1024),
    )(*args)


def matmul(x, w):
    return jnp.dot(x, w, preferred_element_type=F32).astype(BF16)


def apart(x, sites, store):
    head = x.shape[1] // H
    rows = [x[r : r + sites, :] for r in range(0, x.shape[0], sites)]
    for r in range(0, len(rows), 2):
        for h in range(H):
            lanes = slice(h * head, (h + 1) * head)
            pair = [rows[r][:, lanes], rows[r + 1][:, lanes]]
            store(h, r * head, jnp.concatenate(pair, axis=1))


def keep_apart(x, sites, out, blocks=1, block=0):
    def store(h, lane, pair):
        at = (h * blocks + block) * sites
        out[at : at + sites, lane : lane + pair.shape[1]] = pair

    apart(x, sites, store)


def against(probe, keys):
    return lax.dot_general(probe, keys, (((1,), (1,)), ((), ())), preferred_element_type=F32)


def gray(n):
    return n ^ (n >> 1)


def ring_place(other=0):
    place = lax.bitwise_xor(lax.rem(lax.axis_index("seq"), GROUP), other)
    return lax.bitwise_xor(place, lax.shift_right_logical(place, 1))


def kernel_part(count, other, x, out, sems):
    place = lax.axis_index("res") // 2
    start = (1 - place if other else place) * count
    piece = count // sems.shape[0]
    copies = [
        pltpu.make_async_copy(
            x.at[pl.ds(start + n * piece, piece)], out.at[pl.ds(n * piece, piece)], sems.at[n]
        )
        for n in range(sems.shape[0])
    ]
    for copy in copies:
        copy.start()
    for copy in copies:
        copy.wait()


def kernel_near(rows, sites, own, twin, wq, wk, wv, kept, q, k, v, near, x_own, x_twin, sems):
    embed = wq.shape[0]
    moves = [(own, x_own), (twin, x_twin)]
    moves += [(w, kept.at[pl.ds(n * embed, embed)]) for n, w in enumerate((wq, wk, wv))]
    own_in, twin_in, wq_in, wk_in, wv_in = copies = [
        pltpu.make_async_copy(source, target, sems.at[n])
        for n, (source, target) in enumerate(moves)
    ]
    for n in (2, 0, 3, 1, 4):
        copies[n].start()
    wq_in.wait()
    own_in.wait()
    keep_apart(matmul(x_own[...], kept[:embed, :]), sites, q)
    wk_in.wait()
    keep_apart(matmul(x_own[...], kept[embed : 2 * embed, :]), sites, k, 2, 0)
    twin_in.wait()
    keep_apart(matmul(x_twin[...], kept[embed : 2 * embed, :]), sites, k, 2, 1)
    for h in range(H):
        mine, both = slice(h * sites, (h + 1) * sites), slice(2 * h * sites, 2 * (h + 1) * sites)
        near[mine, :] = against(q[mine, :], k[both, :])
    wv_in.wait()
    keep_apart(matmul(x_own[...], kept[2 * embed :, :]), sites, v, 2, 0)
    keep_apart(matmul(x_twin[...], kept[2 * embed :, :]), sites, v, 2, 1)


def rows_that_came(half_width):
    came = (1 - lax.axis_index("res") // 2) * half_width
    return pl.ds(pl.multiple_of(came, half_width), half_width)


def kernel_back(sites, x_far, kept, k, back, q_far, total):
    embed, came = x_far.shape[1], rows_that_came(q_far.shape[1])
    keep_apart(matmul(x_far[...], kept[:embed, :]), sites, q_far)
    for h in range(H):
        mine, both = slice(h * sites, (h + 1) * sites), slice(2 * h * sites, 2 * (h + 1) * sites)
        total[mine, :] = against(q_far[mine, :], k[both, came])
    half = total.shape[0] // 2
    back[...] = jnp.concatenate([total[:half, :], total[half:, :]], axis=1)


def kernel_ahead(sites, x_far, x_far_twin, kept, q, ahead, k_far, k_twin):
    embed, came = x_far_twin.shape[1], rows_that_came(k_far.shape[1])
    keep_apart(matmul(x_far[...], kept[embed : 2 * embed, :]), sites, k_far)
    keep_apart(matmul(x_far_twin[...], kept[embed : 2 * embed, :]), sites, k_twin)
    for h in range(H):
        mine = slice(h * sites, (h + 1) * sites)
        keys = jnp.concatenate([k_far[mine, :], k_twin[mine, :]], axis=0)
        ahead[mine, :] = against(q[mine, came], keys)


def kernel_mix(near, ahead, back, *refs):
    *parts, total = refs
    half = near.shape[0] // 2
    for rows, lanes in (
        (slice(0, half), slice(0, near.shape[1])),
        (slice(half, 2 * half), slice(near.shape[1], 2 * near.shape[1])),
    ):
        far = ahead[rows, :] + back[:, lanes]
        total[rows, :] = jnp.concatenate([near[rows, :], far], axis=1)
    me, size = ring_place(), total.shape[0] // GROUP
    for n, part in enumerate(parts):
        part[...] = total[pl.ds(lax.rem(me + n, GROUP) * size, size), :]


def kernel_sum(a, b, c, d, out):
    out[...] = (a[...] + b[...]) + (c[...] + d[...])


def kernel_softmax(scale, mine, other, out):
    logits = (mine[...] + other[...]) * scale
    e = jnp.exp(logits - jnp.max(logits, axis=1, keepdims=True))
    out[...] = (e / jnp.sum(e, axis=1, keepdims=True)).astype(BF16)


def kernel_values(sites, x, x_twin, kept, out):
    w = kept[2 * x.shape[1] :, :]
    keep_apart(matmul(x[...], w), sites, out, 2, 0)
    keep_apart(matmul(x_twin[...], w), sites, out, 2, 1)


def kernel_last(sites, p0, p1, p2, p3, v_near, v_first, v_second, wo, out, probs, att, mixed, sems):
    place = lax.axis_index("res") // 2
    size, width = H * sites // GROUP, v_first.shape[1]
    head = wo.shape[0] // H
    for n, p in enumerate((p0, p1, p2, p3)):
        probs[pl.ds(ring_place(n) * size, size), :] = p[...]
    rows, halves = out.shape[0] // 2, (1 - place, place)
    for n, far in enumerate((v_first, v_second)):
        came = pl.ds(pl.multiple_of(halves[n] * width, width), width)
        for h in range(0, H, 2):
            pair = []
            for one in (h, h + 1):
                both = slice(2 * one * sites, 2 * (one + 1) * sites)
                v = jnp.concatenate([v_near[both, came], far[both, :]], axis=0)
                p = probs[one * sites : (one + 1) * sites, :]
                pair.append(matmul(p, v))
            for r in range(width // head):
                lanes, to = slice(r * head, (r + 1) * head), n * rows + r * sites
                att[to : to + sites, h * head : (h + 2) * head] = jnp.concatenate(
                    [pair[0][:, lanes], pair[1][:, lanes]], axis=1
                )
    copies = []
    piece = 2 * wo.shape[1] // sems.shape[0]
    for start in range(0, wo.shape[1], piece):
        lanes = slice(start, start + piece)
        mixed[:, lanes] = matmul(att[...], wo[:, lanes])
        for n, half in enumerate(halves):
            source = mixed.at[n * rows : (n + 1) * rows, lanes]
            target = out.at[pl.ds(half * rows, rows), lanes]
            copies.append(pltpu.make_async_copy(source, target, sems.at[len(copies)]))
            copies[-1].start()
    for copy in copies:
        copy.wait()


def swap(x, axis, bit):
    count = lax.axis_size(axis)
    return lax.ppermute(x, axis, [(i, i ^ bit) for i in range(count)])


def turn(x, steps):
    count = lax.axis_size("seq")
    to = [s // GROUP * GROUP + gray((gray(s % GROUP) + steps) % GROUP) for s in range(count)]
    return lax.ppermute(x, "seq", list(enumerate(to)))


def body(x, wq, wk, wv, wo):
    rows, sites, embed = x.shape
    half, head = rows // 2, embed // H
    n_seq = lax.axis_size("seq")
    scale = 1.0 / math.sqrt(head * rows * n_seq)
    flat, half_flat = (rows * sites, embed), (half * sites, embed)
    own = x.reshape(flat)
    cost = 2 * rows * sites * embed * embed

    def part(x, other):
        return call(
            functools.partial(kernel_part, half * sites, other),
            [(half_flat, BF16)],
            (x,),
            scratch=[pltpu.SemaphoreType.DMA((GROUP,))],
            space=pltpu.HBM,
        )[0]

    sent_first = part(own, False)
    far_first = swap(sent_first, "res", 2)
    mine, sent_first = lax.optimization_barrier((own, sent_first))
    twin = swap(mine, "res", 1)
    sums = ((H * sites, 2 * sites), F32)

    def heads(blocks, count):
        return ((H * blocks * sites, count * head), BF16)

    size = H * sites // GROUP
    share = ((size, 4 * sites), F32)
    kept, q, k, v_near, near = call(
        functools.partial(kernel_near, rows, sites),
        [((3 * embed, embed), BF16), heads(1, rows), heads(2, rows), heads(2, rows), sums],
        (own, twin, wq, wk, wv),
        6 * cost,
        [pltpu.VMEM(flat, BF16), pltpu.VMEM(flat, BF16), pltpu.SemaphoreType.DMA((5,))],
        pltpu.HBM,
    )
    later, kept = lax.optimization_barrier((own, kept))
    sent_second = part(later, True)
    far_first, kept, sent_second = lax.optimization_barrier((far_first, kept, sent_second))
    far_first_twin = swap(far_first, "res", 1)
    (sent_back,) = call(
        functools.partial(kernel_back, sites),
        [((H * sites // 2, 4 * sites), F32)],
        (far_first, kept, k),
        cost,
        [pltpu.VMEM(*heads(1, half)), pltpu.VMEM(*sums)],
    )
    back = swap(sent_back, "res", 2)
    far_first_twin, sent_back, sent_second = lax.optimization_barrier(
        (far_first_twin, sent_back, sent_second)
    )
    far_second = swap(sent_second, "res", 2)
    (ahead,) = call(
        functools.partial(kernel_ahead, sites),
        [sums],
        (far_first, far_first_twin, kept, q),
        cost,
        [pltpu.VMEM(*heads(1, half)), pltpu.VMEM(*heads(1, half))],
    )
    wide = ((H * sites, 4 * sites), F32)
    far = call(kernel_mix, [share] * GROUP, (near, ahead, back), 0, [pltpu.VMEM(*wide)])
    far = [far[0]] + [turn(far[n], n) for n in (2, 1, 3)]
    far[1], kept = lax.optimization_barrier((far[1], kept))
    (v_first,) = call(
        functools.partial(kernel_values, sites),
        [heads(2, half)],
        (far_first, far_first_twin, kept),
        cost,
    )
    far[2], v_first = lax.optimization_barrier((far[2], v_first))
    (mine,) = call(kernel_sum, [share], far)
    (probs,) = call(
        functools.partial(kernel_softmax, scale),
        [((size, 4 * sites), BF16)],
        (mine, swap(mine, "seq", GROUP)),
        2000000000,
    )
    far_second, probs = lax.optimization_barrier((far_second, probs))
    far_second_twin = swap(far_second, "res", 1)
    others = [swap(probs, "seq", k) for k in range(1, GROUP)]

    (v_second,) = call(
        functools.partial(kernel_values, sites),
        [heads(2, half)],
        (far_second, far_second_twin, kept),
        cost,
    )
    (out,) = call(
        functools.partial(kernel_last, sites),
        [(flat, BF16)],
        (probs, *others, v_near, v_first, v_second, wo),
        2 * cost,
        [
            pltpu.VMEM((H * sites, 4 * sites), BF16),
            pltpu.VMEM(flat, BF16),
            pltpu.VMEM(flat, BF16),
            pltpu.SemaphoreType.DMA((2 * H // GROUP,)),
        ],
        to=pltpu.HBM,
    )
    return out.reshape(rows, sites, embed)


def solution(mesh):
    placed = (P("seq", "res", None), P(), P(), P(), P())
    fits = mesh.shape["res"] == 4 and mesh.shape["seq"] == 2 * GROUP
    return jax.shard_map(
        body if fits else plain_body,
        mesh=mesh,
        in_specs=placed,
        out_specs=P("seq", "res", None),
        check_vma=False,
    )
```

```python
import functools
import math

import jax
import jax.numpy as jnp
from jax import lax
from jax.experimental import pallas as pl
from jax.experimental.pallas import tpu as pltpu
from jax.sharding import PartitionSpec as P

H = 12
GROUP = 4
F32, BF16 = jnp.float32, jnp.bfloat16


def reshape_by_group(inputs, weight, attention_groups):
    sequence_number, site_number, embed_size = inputs.shape
    out = jnp.dot(
        inputs.reshape(sequence_number * site_number, embed_size),
        weight,
        preferred_element_type=F32,
    )
    return out.astype(BF16).reshape(
        sequence_number, site_number, attention_groups, embed_size // attention_groups
    )


def plain_body(
    alignment_embedding, probe_projector, lookup_projector, content_projector, final_projector
):
    sequence_number, site_number, embed_size = alignment_embedding.shape
    head_size = embed_size // H
    scale = 1.0 / math.sqrt(head_size * sequence_number * lax.axis_size("seq"))
    probe_tensor = reshape_by_group(alignment_embedding, probe_projector, H)
    gathered = lax.all_gather(alignment_embedding, "res", axis=1, tiled=True)
    all_keys = reshape_by_group(gathered, lookup_projector, H)
    all_values = reshape_by_group(gathered, content_projector, H)
    logits = jnp.einsum("rihe,rjhe->hij", probe_tensor, all_keys, preferred_element_type=F32)
    summed = lax.psum(logits, "seq")
    probs = jax.nn.softmax(summed * scale, axis=-1).astype(BF16)
    attended = jnp.einsum("hij,rjhe->rihe", probs, all_values, preferred_element_type=F32)
    attended = attended.astype(BF16).reshape(sequence_number * site_number, embed_size)
    mixed = jnp.dot(attended, final_projector, preferred_element_type=F32).astype(BF16)
    return mixed.reshape(sequence_number, site_number, embed_size)


def call(kernel, outs, args, flops=0, scratch=(), space=pltpu.VMEM, to=pltpu.VMEM):
    shapes = [jax.ShapeDtypeStruct(s, d) for s, d in outs]
    if space == pltpu.HBM:
        args = [pltpu.with_memory_space_constraint(a, space) for a in args]
    moved = sum(a.size * a.dtype.itemsize for a in list(args) + shapes)
    return pl.pallas_call(
        kernel,
        out_shape=shapes,
        in_specs=[pl.BlockSpec(memory_space=space)] * len(args),
        out_specs=[pl.BlockSpec(memory_space=to)] * len(shapes),
        scratch_shapes=list(scratch),
        cost_estimate=pl.CostEstimate(flops=flops, bytes_accessed=moved, transcendentals=0),
        compiler_params=pltpu.CompilerParams(vmem_limit_bytes=4 * 1024 * 1024),
    )(*args)


def matmul(x, w):
    return jnp.dot(x, w, preferred_element_type=F32).astype(BF16)


def apart(x, sites, store):
    head = x.shape[1] // H
    rows = [x[r : r + sites, :] for r in range(0, x.shape[0], sites)]
    for r in range(0, len(rows), 2):
        for h in range(H):
            lanes = slice(h * head, (h + 1) * head)
            pair = [rows[r][:, lanes], rows[r + 1][:, lanes]]
            store(h, r * head, jnp.concatenate(pair, axis=1))


def keep_apart(x, sites, out, blocks=1, block=0):
    def store(h, lane, pair):
        at = (h * blocks + block) * sites
        out[at : at + sites, lane : lane + pair.shape[1]] = pair

    apart(x, sites, store)


def against(probe, keys):
    return lax.dot_general(probe, keys, (((1,), (1,)), ((), ())), preferred_element_type=F32)


def gray(n):
    return n ^ (n >> 1)


def ring_place(other=0):
    place = lax.bitwise_xor(lax.rem(lax.axis_index("seq"), GROUP), other)
    return lax.bitwise_xor(place, lax.shift_right_logical(place, 1))


def kernel_part(count, other, x, out, sems):
    place = lax.axis_index("res") // 2
    start = (1 - place if other else place) * count
    piece = count // sems.shape[0]
    copies = [
        pltpu.make_async_copy(
            x.at[pl.ds(start + n * piece, piece)], out.at[pl.ds(n * piece, piece)], sems.at[n]
        )
        for n in range(sems.shape[0])
    ]
    for copy in copies:
        copy.start()
    for copy in copies:
        copy.wait()


def kernel_near(rows, sites, own, twin, wq, wk, wv, kept, q, k, v, near, x_own, x_twin, sems):
    embed = wq.shape[0]
    moves = [(own, x_own), (twin, x_twin)]
    moves += [(w, kept.at[pl.ds(n * embed, embed)]) for n, w in enumerate((wq, wk, wv))]
    own_in, twin_in, wq_in, wk_in, wv_in = copies = [
        pltpu.make_async_copy(source, target, sems.at[n])
        for n, (source, target) in enumerate(moves)
    ]
    for n in (2, 0, 3, 1, 4):
        copies[n].start()
    wq_in.wait()
    own_in.wait()
    keep_apart(matmul(x_own[...], kept[:embed, :]), sites, q)
    wk_in.wait()
    keep_apart(matmul(x_own[...], kept[embed : 2 * embed, :]), sites, k, 2, 0)
    twin_in.wait()
    keep_apart(matmul(x_twin[...], kept[embed : 2 * embed, :]), sites, k, 2, 1)
    for h in range(H):
        mine, both = slice(h * sites, (h + 1) * sites), slice(2 * h * sites, 2 * (h + 1) * sites)
        near[mine, :] = against(q[mine, :], k[both, :])
    wv_in.wait()
    keep_apart(matmul(x_own[...], kept[2 * embed :, :]), sites, v, 2, 0)
    keep_apart(matmul(x_twin[...], kept[2 * embed :, :]), sites, v, 2, 1)


def rows_that_came(half_width):
    came = (1 - lax.axis_index("res") // 2) * half_width
    return pl.ds(pl.multiple_of(came, half_width), half_width)


def kernel_back(sites, x_far, kept, k, back, q_far, total):
    embed, came = x_far.shape[1], rows_that_came(q_far.shape[1])
    keep_apart(matmul(x_far[...], kept[:embed, :]), sites, q_far)
    for h in range(H):
        mine, both = slice(h * sites, (h + 1) * sites), slice(2 * h * sites, 2 * (h + 1) * sites)
        total[mine, :] = against(q_far[mine, :], k[both, came])
    half = total.shape[0] // 2
    back[...] = jnp.concatenate([total[:half, :], total[half:, :]], axis=1)


def kernel_ahead(sites, x_far, x_far_twin, kept, q, ahead, k_far, k_twin):
    embed, came = x_far_twin.shape[1], rows_that_came(k_far.shape[1])
    keep_apart(matmul(x_far[...], kept[embed : 2 * embed, :]), sites, k_far)
    keep_apart(matmul(x_far_twin[...], kept[embed : 2 * embed, :]), sites, k_twin)
    for h in range(H):
        mine = slice(h * sites, (h + 1) * sites)
        keys = jnp.concatenate([k_far[mine, :], k_twin[mine, :]], axis=0)
        ahead[mine, :] = against(q[mine, came], keys)


def kernel_mix(near, ahead, back, *refs):
    *parts, total = refs
    half = near.shape[0] // 2
    for rows, lanes in (
        (slice(0, half), slice(0, near.shape[1])),
        (slice(half, 2 * half), slice(near.shape[1], 2 * near.shape[1])),
    ):
        far = ahead[rows, :] + back[:, lanes]
        total[rows, :] = jnp.concatenate([near[rows, :], far], axis=1)
    me, size = ring_place(), total.shape[0] // GROUP
    for n, part in enumerate(parts):
        part[...] = total[pl.ds(lax.rem(me + n, GROUP) * size, size), :]


def kernel_sum(a, b, c, d, out):
    out[...] = (a[...] + b[...]) + (c[...] + d[...])


def kernel_softmax(scale, mine, other, out):
    logits = (mine[...] + other[...]) * scale
    e = jnp.exp(logits - jnp.max(logits, axis=1, keepdims=True))
    out[...] = (e / jnp.sum(e, axis=1, keepdims=True)).astype(BF16)


def kernel_values(sites, x, x_twin, kept, out):
    w = kept[2 * x.shape[1] :, :]
    keep_apart(matmul(x[...], w), sites, out, 2, 0)
    keep_apart(matmul(x_twin[...], w), sites, out, 2, 1)


def kernel_last(sites, p0, p1, p2, p3, v_near, v_first, v_second, wo, out, probs, att, mixed, sems):
    place = lax.axis_index("res") // 2
    size, width = H * sites // GROUP, v_first.shape[1]
    head = wo.shape[0] // H
    for n, p in enumerate((p0, p1, p2, p3)):
        probs[pl.ds(ring_place(n) * size, size), :] = p[...]
    rows, halves = out.shape[0] // 2, (1 - place, place)
    for n, far in enumerate((v_first, v_second)):
        came = pl.ds(pl.multiple_of(halves[n] * width, width), width)
        for h in range(0, H, 2):
            pair = []
            for one in (h, h + 1):
                both = slice(2 * one * sites, 2 * (one + 1) * sites)
                v = jnp.concatenate([v_near[both, came], far[both, :]], axis=0)
                p = probs[one * sites : (one + 1) * sites, :]
                pair.append(matmul(p, v))
            for r in range(width // head):
                lanes, to = slice(r * head, (r + 1) * head), n * rows + r * sites
                att[to : to + sites, h * head : (h + 2) * head] = jnp.concatenate(
                    [pair[0][:, lanes], pair[1][:, lanes]], axis=1
                )
    copies = []
    piece = 2 * wo.shape[1] // sems.shape[0]
    for start in range(0, wo.shape[1], piece):
        lanes = slice(start, start + piece)
        mixed[:, lanes] = matmul(att[...], wo[:, lanes])
        for n, half in enumerate(halves):
            source = mixed.at[n * rows : (n + 1) * rows, lanes]
            target = out.at[pl.ds(half * rows, rows), lanes]
            copies.append(pltpu.make_async_copy(source, target, sems.at[len(copies)]))
            copies[-1].start()
    for copy in copies:
        copy.wait()


def swap(x, axis, bit):
    count = lax.axis_size(axis)
    return lax.ppermute(x, axis, [(i, i ^ bit) for i in range(count)])


def turn(x, steps):
    count = lax.axis_size("seq")
    to = [s // GROUP * GROUP + gray((gray(s % GROUP) + steps) % GROUP) for s in range(count)]
    return lax.ppermute(x, "seq", list(enumerate(to)))


def body(x, wq, wk, wv, wo):
    rows, sites, embed = x.shape
    half, head = rows // 2, embed // H
    n_seq = lax.axis_size("seq")
    scale = 1.0 / math.sqrt(head * rows * n_seq)
    flat, half_flat = (rows * sites, embed), (half * sites, embed)
    own = x.reshape(flat)
    cost = 2 * rows * sites * embed * embed

    def part(x, other):
        return call(
            functools.partial(kernel_part, half * sites, other),
            [(half_flat, BF16)],
            (x,),
            scratch=[pltpu.SemaphoreType.DMA((1,))],
            space=pltpu.HBM,
        )[0]

    sent_first = part(own, False)
    far_first = swap(sent_first, "res", 2)
    mine, sent_first = lax.optimization_barrier((own, sent_first))
    twin = swap(mine, "res", 1)
    sums = ((H * sites, 2 * sites), F32)

    def heads(blocks, count):
        return ((H * blocks * sites, count * head), BF16)

    size = H * sites // GROUP
    share = ((size, 4 * sites), F32)
    kept, q, k, v_near, near = call(
        functools.partial(kernel_near, rows, sites),
        [((3 * embed, embed), BF16), heads(1, rows), heads(2, rows), heads(2, rows), sums],
        (own, twin, wq, wk, wv),
        6 * cost,
        [pltpu.VMEM(flat, BF16), pltpu.VMEM(flat, BF16), pltpu.SemaphoreType.DMA((5,))],
        pltpu.HBM,
    )
    later, kept = lax.optimization_barrier((own, kept))
    sent_second = part(later, True)
    far_first, kept, sent_second = lax.optimization_barrier((far_first, kept, sent_second))
    far_first_twin = swap(far_first, "res", 1)
    (sent_back,) = call(
        functools.partial(kernel_back, sites),
        [((H * sites // 2, 4 * sites), F32)],
        (far_first, kept, k),
        cost,
        [pltpu.VMEM(*heads(1, half)), pltpu.VMEM(*sums)],
    )
    back = swap(sent_back, "res", 2)
    far_first_twin, sent_back, sent_second = lax.optimization_barrier(
        (far_first_twin, sent_back, sent_second)
    )
    far_second = swap(sent_second, "res", 2)
    (ahead,) = call(
        functools.partial(kernel_ahead, sites),
        [sums],
        (far_first, far_first_twin, kept, q),
        cost,
        [pltpu.VMEM(*heads(1, half)), pltpu.VMEM(*heads(1, half))],
    )
    wide = ((H * sites, 4 * sites), F32)
    far = call(kernel_mix, [share] * GROUP, (near, ahead, back), 0, [pltpu.VMEM(*wide)])
    far = [far[0]] + [turn(far[n], n) for n in (2, 1, 3)]
    far[1], kept = lax.optimization_barrier((far[1], kept))
    (v_first,) = call(
        functools.partial(kernel_values, sites),
        [heads(2, half)],
        (far_first, far_first_twin, kept),
        cost,
    )
    far[2], v_first = lax.optimization_barrier((far[2], v_first))
    (mine,) = call(kernel_sum, [share], far)
    (probs,) = call(
        functools.partial(kernel_softmax, scale),
        [((size, 4 * sites), BF16)],
        (mine, swap(mine, "seq", GROUP)),
        2000000000,
    )
    far_second, probs = lax.optimization_barrier((far_second, probs))
    far_second_twin = swap(far_second, "res", 1)
    others = [swap(probs, "seq", k) for k in range(1, GROUP)]

    (v_second,) = call(
        functools.partial(kernel_values, sites),
        [heads(2, half)],
        (far_second, far_second_twin, kept),
        cost,
    )
    (out,) = call(
        functools.partial(kernel_last, sites),
        [(flat, BF16)],
        (probs, *others, v_near, v_first, v_second, wo),
        2 * cost,
        [
            pltpu.VMEM((H * sites, 4 * sites), BF16),
            pltpu.VMEM(flat, BF16),
            pltpu.VMEM(flat, BF16),
            pltpu.SemaphoreType.DMA((2 * H // GROUP,)),
        ],
        to=pltpu.HBM,
    )
    return out.reshape(rows, sites, embed)


def solution(mesh):
    placed = (P("seq", "res", None), P(), P(), P(), P())
    fits = mesh.shape["res"] == 4 and mesh.shape["seq"] == 2 * GROUP
    return jax.shard_map(
        body if fits else plain_body,
        mesh=mesh,
        in_specs=placed,
        out_specs=P("seq", "res", None),
        check_vma=False,
    )
```
